32 devices in a mesh: row: 8 (over z, x), col: 4 (over y, core).
Axes of the slice: x: 2, y: 2, z: 4, core: 2. Of those that a mesh axis runs over, the one named last changes fastest.
Arguments:
- anc_inv: bfloat16 [16384, 16384], P('row', 'col'), may hold values from -0.0546875 to 0.0546875
- panel: bfloat16 [1, 12288, 2048], P(None, 'col', 'row'), may hold values from -6 to 6
- structure: int32 [1, 96], replicated, may hold values from 0 to 127, as said below
Outputs:
- off_inv: float32 [1, 16384, 2048], P(None, 'row', 'col')
The draws below stay inside these ranges and needn't reach their ends.
Inputs may be any that keep to these rules, and one draw needn't show every extreme that they name: Each structure[s] holds 96 distinct ancestor block indices, in the order in which the panel stores its row blocks (not sorted); each group of 32 consecutive ancestor blocks holds 23 to 25 of them, and some group of each supernode holds exactly 25.
All inputs are finite; a program needn't handle non-finite values.
Results may differ from the reference program's by a relative error of at most 0.0003.
Values may be sent and summed in bfloat16 or wider, within the bound.
A program may use at most 128 MiB of HBM per device.

```python
import jax
import jax.numpy as jnp
from jax import lax

BS = 128
W = 2048
SBLK = 96
NAB = 128
NSUP = 1
NA = 16384
SROWS = 12288
GROUP = 32
CAP = 25
N_COL = 4


def draw_structure(key, part):
    col_count = NAB // GROUP
    pair_count = col_count // 2
    mean_count = CAP - 1
    rows_out = []
    for supernode in range(NSUP):
        sub_key = jax.random.fold_in(key, 101 + supernode)
        key_pairs, key_first, key_order, key_ranks, key_shuffle = jax.random.split(sub_key, 5)
        choose = jax.random.randint(key_pairs, (pair_count,), 0, 3)
        forced = jax.random.randint(key_first, (1,), 0, 2) * 2
        choose = jnp.concatenate([forced, choose[1:]])
        counts = jnp.stack([mean_count - 1 + choose, mean_count + 1 - choose], axis=1).reshape(col_count)
        counts = jax.random.permutation(key_order, counts)
        ordinal = jax.vmap(lambda branch_key: jax.random.permutation(branch_key, GROUP))(jax.random.split(key_ranks, col_count))
        chosen = (ordinal < counts[:, None]).reshape(NAB)
        scores = jnp.where(chosen, 0, NAB) + jnp.arange(NAB, dtype=jnp.int32)
        ordering = jnp.argsort(scores, stable=True)[:SBLK].astype(jnp.int32)
        shuffled = jax.random.permutation(key_shuffle, ordering)
        rows_out.append(shuffled.astype(jnp.int32))
    return jnp.stack(rows_out)


def shard_levels(own_key, shape, cuts, low, high):
    def one(dim, parts):
        steps = jax.random.uniform(jax.random.fold_in(jax.random.fold_in(own_key, 6), dim), (parts,), jnp.float32, low / len(cuts), high / len(cuts))
        return jnp.repeat(jnp.exp(steps), shape[dim] // parts).reshape((-1,) + (1,) * (len(shape) - dim - 1))

    gain = one(*cuts[0])
    for cut in cuts[1:]:
        gain = gain * one(*cut)
    return gain


def scatter_about(key, dims, scale, most, shards=(), held_as=jnp.bfloat16):
    factor_of = shard_levels(key, dims, shards, -0.22, 0.18) if shards else 1.0
    values = jax.random.normal(key, dims, jnp.float32) * scale * factor_of
    return jnp.minimum(jnp.maximum(values, -most), most).astype(held_as)


def setup_inputs(seed: int = 0) -> dict:
    arg_keys = jax.random.split(jax.random.key(seed), 4)
    return {
        "anc_inv": scatter_about(arg_keys[0], (NA, NA), SROWS ** -0.5, 0.0546875, ((0, 8), (1, 4))),
        "panel": scatter_about(arg_keys[1], (NSUP, SROWS, W), 1.0, 6.0, ((1, 4), (2, 8))),
        "structure": draw_structure(jax.random.fold_in(arg_keys[3], 71), 0),
    }


def reference(anc_inv, panel, structure):
    group_blocks = NAB // N_COL
    ancestors = jnp.arange(NAB, dtype=jnp.int32)
    results = []
    for supernode in range(NSUP):
        onehot = structure[supernode][None, :] == ancestors[:, None]
        compact = panel[supernode].astype(jnp.float32).reshape(SBLK, BS * W)
        expanded = jnp.dot(onehot.astype(jnp.float32), compact, precision=lax.Precision.HIGHEST).reshape(NAB * BS, W)

        def add_group(group_index, total):
            offset = (group_index * (group_blocks * BS)).astype(jnp.int32)
            columns = lax.dynamic_slice_in_dim(anc_inv, offset, group_blocks * BS, 1).astype(jnp.float32)
            rows_part = lax.dynamic_slice_in_dim(expanded, offset, group_blocks * BS, 0)
            partial_value = jnp.dot(columns, rows_part, precision=lax.Precision.HIGHEST)
            return total + partial_value

        total = lax.fori_loop(0, N_COL, add_group, jnp.zeros((NAB * BS, W), jnp.float32))
        member = jnp.repeat(jnp.any(onehot, axis=1), BS)
        results.append(jnp.where(member[:, None], -total, jnp.zeros_like(total)))
    return jnp.stack(results)
```

```python
import functools

import jax
import jax.numpy as jnp
from jax import lax
from jax.experimental import pallas as pl
from jax.experimental.pallas import tpu as pltpu
from jax.sharding import PartitionSpec as P

BS = 128
MESH = pl.DeviceIdType.MESH


def kernel(dims, ids, pos, a_hbm, panel_hbm, out_ref,
           G, E, AC, abufs, S, SS, R, RS,
           l_sem, a_sem, g_send, g_recv, e_send, e_recv, r_send, r_recv, rs_send, rs_recv):
    NZ, NX, NC, CAP, H, MB = dims
    NR = NZ * NX
    J = NR // NC
    NCH = NC // 2
    r = lax.axis_index("row")
    c = lax.axis_index("col")
    z, x = r // NX, r % NX
    m, k = c // 2, c % 2
    sibling = m * 2 + 1 - k
    M, K = AC.shape
    w = E.shape[2]
    wh = w // H
    PB = panel_hbm.shape[1]
    GB, RB = abufs[0].shape[:2]
    i32 = lambda v: v.astype(jnp.int32)
    nbrs = [(z + 1 < NZ, r + NX), (z > 0, r - NX), (x + 1 < NX, r + 1), (x > 0, r - 1)]

    def panel_copy(h):
        return pltpu.make_async_copy(
            panel_hbm.at[0, :, :, pl.ds(h * wh, wh)], G[h].at[pl.ds(c * PB, PB)], l_sem.at[h])

    def a_copies(i, b):
        rows = pl.ds(pl.multiple_of(i * RB, RB), RB)
        return [pltpu.make_async_copy(a_hbm.at[rows, pl.ds(q * BS, BS)], abufs[b].at[q], a_sem.at[b, q])
                for q in range(GB)]

    for h in range(H):
        panel_copy(h).start()
    for cp in a_copies(0, 0):
        cp.start()

    barrier = pltpu.get_barrier_semaphore()
    for dc in range(1, NC):
        pl.semaphore_signal(barrier, inc=1, device_id={"col": (c + dc) % NC}, device_id_type=MESH)
    for ok, dev in nbrs:
        @pl.when(ok)
        def _(dev=dev):
            pl.semaphore_signal(barrier, inc=1, device_id={"row": dev}, device_id_type=MESH)
    pl.semaphore_wait(barrier, NC - 1 + sum(i32(ok) for ok, _ in nbrs))

    for h in range(H):
        G[h][NC * PB] = jnp.zeros((BS, wh), jnp.bfloat16)

    def g_copy(h, src, dst, idx):
        blk = G[h].at[pl.ds(src * PB, PB)]
        return pltpu.make_async_remote_copy(
            src_ref=blk, dst_ref=blk, send_sem=g_send.at[h, idx], recv_sem=g_recv.at[h, src],
            device_id={"col": dst}, device_id_type=MESH)

    for h in range(H):
        panel_copy(h).wait()
        for dm in range(1, NCH):
            g_copy(h, c, (m + dm) % NCH * 2 + k, dm - 1).start()
        g_copy(h, c, sibling, NCH - 1).start()

    NA_CH = M // RB

    def pack(p, carry):
        for b in range(2):
            i = p * 2 + b

            @pl.when(i + 1 < NA_CH)
            def _():
                for cp in a_copies(i + 1, 1 - b):
                    cp.start()
            for cp in a_copies(i, b):
                cp.wait()
            rows = pl.ds(pl.multiple_of(i * RB, RB), RB)
            for q in range(CAP):
                AC[rows, q * BS:(q + 1) * BS] = abufs[b][ids[q]]
        return carry

    lax.fori_loop(0, NA_CH // 2, pack, 0)

    def e_copy(j, h, dev, d):
        blk = E.at[j, :, pl.ds(h * wh, wh)]
        return pltpu.make_async_remote_copy(
            src_ref=blk, dst_ref=blk, send_sem=e_send.at[j, h, d], recv_sem=e_recv.at[j, h],
            device_id={"row": dev}, device_id_type=MESH)

    def flags(j):
        zs, xs = j // NX, j % NX
        own = xs == x
        return [own & (zs <= z) & (z + 1 < NZ), own & (zs >= z) & (z > 0),
                (xs <= x) & (x + 1 < NX), (xs >= x) & (x > 0)]

    def forward(j, h, act):
        for d in (2, 3, 0, 1):
            @pl.when(flags(j)[d])
            def _(d=d):
                act(e_copy(j, h, nbrs[d][1], d))

    def slot_of(j):
        return (j - (c + 1) * J + 2 * NR) % NR

    def r_copies(j):
        d, jj = j // J, j % J
        slot = slot_of(j)
        rel = (c - d - 1 + NC) % NC
        return [pltpu.make_async_remote_copy(
            src_ref=a.at[slot], dst_ref=b.at[rel, jj], send_sem=s.at[slot], recv_sem=t.at[rel, jj],
            device_id={"col": d}, device_id_type=MESH)
            for a, b, s, t in ((S, R, r_send, r_recv), (SS, RS, rs_send, rs_recv))]

    def compute(j):
        own = j // J == c
        slot = slot_of(j)

        def chunk(i, carry):
            rows = pl.ds(pl.multiple_of(i * MB, MB), MB)
            prod = jnp.dot(AC[rows, :], E[j], preferred_element_type=jnp.float32)
            for jj in range(J):
                @pl.when(j == c * J + jj)
                def _(jj=jj):
                    out_ref[rows, jj * w:(jj + 1) * w] = prod

            @pl.when(jnp.logical_not(own))
            def _():
                top = jnp.maximum(jnp.max(jnp.abs(prod), axis=0, keepdims=True), 1e-30)
                SS[slot, pl.ds(i, 1), :] = top * (1.0 / 32767.0)
                S[slot, rows, :] = jnp.round(prod * (32767.0 / top)).astype(jnp.int16)
            return carry

        lax.fori_loop(0, M // MB, chunk, 0)

        @pl.when(jnp.logical_not(own))
        def _():
            for cp in r_copies(j):
                cp.start()

    for h in range(H):
        for dm in range(1, NCH):
            src = (m + dm) % NCH * 2 + k
            g_copy(h, src, sibling, 0).wait_recv()
            g_copy(h, src, sibling, NCH - 1 + dm).start()
        for dm in range(NCH):
            g_copy(h, (m + dm) % NCH * 2 + 1 - k, sibling, 0).wait_recv()
        for q in range(CAP):
            E[r, q * BS:(q + 1) * BS, h * wh:(h + 1) * wh] = G[h][pos[q]]
        forward(r, h, lambda cp: cp.start())
    compute(r)

    def zorder(i):
        near = jnp.minimum(z, NZ - 1 - z)
        t = (i + 1) // 2
        two = jnp.where(i % 2 == 1, z - t, z + t)
        one = jnp.where(z < NZ - 1 - z, z + (i - near), z - (i - near))
        return jnp.where(i <= 2 * near, two, one)

    def xorder(i):
        near = jnp.minimum(x, NX - 1 - x)
        t = (i + 1) // 2
        two = jnp.where(i % 2 == 1, x - t, x + t)
        one = jnp.where(x < NX - 1 - x, x + (i - near), x - (i - near))
        return jnp.where(i <= 2 * near, two, one)

    def step(s, carry):
        if NX == 2:
            last = s == 2 * NZ - 1
            d = jnp.where(last, 1, (s + 1) % 2)
            zi = jnp.where(last, NZ - 1, jnp.where(s % 2 == 1, (s + 1) // 2, s // 2 - 1))
            j = zorder(zi) * NX + jnp.where(d == 1, 1 - x, x)
        else:
            j = zorder(s // NX) * NX + xorder(s % NX)
        for h in range(H):
            e_copy(j, h, nbrs[0][1], 0).wait_recv()
            forward(j, h, lambda cp: cp.start())
        compute(j)
        return carry

    lax.fori_loop(1, NR, step, 0)

    for rel in range(NC - 1):
        for jj in range(J):
            for src, dst, s, t in ((S, R, r_send, r_recv), (SS, RS, rs_send, rs_recv)):
                pltpu.make_async_remote_copy(
                    src_ref=src.at[0], dst_ref=dst.at[rel, jj], send_sem=s.at[0], recv_sem=t.at[rel, jj],
                    device_id={"col": sibling}, device_id_type=MESH).wait_recv()
    for jj in range(J):
        def add(i, carry, jj=jj):
            rows = pl.ds(pl.multiple_of(i * MB, MB), MB)
            total = out_ref[rows, jj * w:(jj + 1) * w]
            for rel in range(NC - 1):
                total += R[rel, jj, rows, :].astype(jnp.float32) * RS[rel, jj, pl.ds(i, 1), :]
            out_ref[rows, jj * w:(jj + 1) * w] = total
            return carry
        lax.fori_loop(0, M // MB, add, 0)

    for h in range(H):
        for idx in range(NC - 1):
            g_copy(h, c, sibling, idx).wait_send()

    def drain(j, carry):
        for h in range(H):
            forward(j, h, lambda cp: cp.wait_send())

        @pl.when(j // J != c)
        def _():
            for cp in r_copies(j):
                cp.wait_send()
        return carry

    lax.fori_loop(0, NR, drain, 0)


def body(NR, NC, anc_inv, panel, structure):
    c = lax.axis_index("col")
    r = lax.axis_index("row")
    M, cols = anc_inv.shape
    GB = cols // BS
    CAP = GB * 3 // 4 + 1
    PB, w = panel.shape[1] // BS, panel.shape[2]
    NX = 2
    while NX * NX * 2 < NR:
        NX *= 2
    NZ = NR // NX
    H = max(1, w // 128)
    wh = w // H
    J = NR // NC
    MB = 256
    RB = 256
    K = CAP * BS
    s = structure[0]
    n = s.shape[0]
    at = jnp.arange(n, dtype=jnp.int32)
    mine = s // GB == c
    rank = jnp.sum((at[None, :] < at[:, None]) & mine[None, :], axis=1)
    hot = mine[None, :] & (rank[None, :] == jnp.arange(CAP)[:, None])
    pos = n + jnp.sum(jnp.where(hot, at[None, :] - n, 0), axis=1).astype(jnp.int32)
    ids = jnp.sum(jnp.where(hot, (s - c * GB)[None, :], 0), axis=1).astype(jnp.int32)
    D = pltpu.SemaphoreType.DMA
    chunks = max(8, M // MB)
    smem = pl.BlockSpec(memory_space=pltpu.SMEM)
    hbm = pl.BlockSpec(memory_space=pl.ANY)
    total = pl.pallas_call(
        functools.partial(kernel, (NZ, NX, NC, CAP, H, MB)),
        out_shape=jax.ShapeDtypeStruct((M, J * w), jnp.float32),
        in_specs=[smem, smem, hbm, hbm],
        out_specs=pl.BlockSpec(memory_space=pltpu.VMEM),
        scratch_shapes=[
            [pltpu.VMEM((NC * PB + 1, BS, wh), jnp.bfloat16)] * H,
            pltpu.VMEM((NR, K, w), jnp.bfloat16),
            pltpu.VMEM((M, K), jnp.bfloat16),
            [pltpu.VMEM((GB, RB, BS), jnp.bfloat16)] * 2,
            pltpu.VMEM((NR - J, M, w), jnp.int16),
            pltpu.VMEM((NR - J, chunks, w), jnp.float32),
            pltpu.VMEM((NC - 1, J, M, w), jnp.int16),
            pltpu.VMEM((NC - 1, J, chunks, w), jnp.float32),
            D((H,)), D((2, GB)), D((H, NC - 1)), D((H, NC)), D((NR, H, 4)), D((NR, H)),
            D((NR - J,)), D((NC - 1, J)), D((NR - J,)), D((NC - 1, J)),
        ],
        compiler_params=pltpu.CompilerParams(
            collective_id=0, has_side_effects=True, vmem_limit_bytes=63 * 2**20),
    )(ids, pos, anc_inv, panel.reshape(1, PB, BS, w))
    own_blocks = r * (M // BS) + jnp.arange(M // BS, dtype=jnp.int32)
    member = jnp.any(s[None, :] == own_blocks[:, None], axis=1)
    mask = jnp.repeat(member, BS)
    return jnp.where(mask[:, None], -total, 0.0)[None]


def solution(mesh):
    in_specs = (P("row", "col"), P(None, "col", "row"), P())
    out_specs = P(None, "row", "col")
    fn = functools.partial(body, mesh.shape["row"], mesh.shape["col"])
    return jax.shard_map(fn, mesh=mesh, in_specs=in_specs, out_specs=out_specs, check_vma=False)
```

```python
import functools

import jax
import jax.numpy as jnp
from jax import lax
from jax.experimental import pallas as pl
from jax.experimental.pallas import tpu as pltpu
from jax.sharding import PartitionSpec as P

BS = 128
MESH = pl.DeviceIdType.MESH


def kernel(dims, ids, pos, a_hbm, panel_hbm, out_ref,
           G, E, AC, abufs, Y, far_bufs, mate_bufs, half_bufs,
           l_sem, a_sem, g_send, g_recv, e_send, e_recv, far_sems, mate_sems, half_sems):
    NZ, NX, NC, CAP, H, MB, MM, KA = dims
    NR = NZ * NX
    J = NR // NC
    NCH = NC // 2
    r = lax.axis_index("row")
    c = lax.axis_index("col")
    z, x = r // NX, r % NX
    m, k = c // 2, c % 2
    sibling = m * 2 + 1 - k
    M, K = AC.shape
    HM = M // 2
    w = E.shape[2]
    wh = w // H
    PB = panel_hbm.shape[1]
    GB, RB = abufs[0].shape[:2]
    i32 = lambda v: v.astype(jnp.int32)
    nbrs = [(z + 1 < NZ, r + NX), (z > 0, r - NX), (x + 1 < NX, r + 1), (x > 0, r - 1)]

    def panel_copy(h):
        return pltpu.make_async_copy(
            panel_hbm.at[0, :, :, pl.ds(h * wh, wh)], G[h].at[pl.ds(c * PB, PB)], l_sem.at[h])

    def a_copies(i, b):
        rows = pl.ds(pl.multiple_of(i * RB, RB), RB)
        return [pltpu.make_async_copy(a_hbm.at[rows, pl.ds(q * BS, BS)], abufs[b].at[q], a_sem.at[b, q])
                for q in range(GB)]

    for h in range(H):
        panel_copy(h).start()
    for cp in a_copies(0, 0):
        cp.start()

    barrier = pltpu.get_barrier_semaphore()
    for dc in range(1, NC):
        pl.semaphore_signal(barrier, inc=1, device_id={"col": (c + dc) % NC}, device_id_type=MESH)
    for ok, dev in nbrs:
        @pl.when(ok)
        def _(dev=dev):
            pl.semaphore_signal(barrier, inc=1, device_id={"row": dev}, device_id_type=MESH)
    pl.semaphore_wait(barrier, NC - 1 + sum(i32(ok) for ok, _ in nbrs))

    for h in range(H):
        G[h][NC * PB] = jnp.zeros((BS, wh), jnp.bfloat16)

    def g_copy(h, src, dst, idx):
        blk = G[h].at[pl.ds(src * PB, PB)]
        return pltpu.make_async_remote_copy(
            src_ref=blk, dst_ref=blk, send_sem=g_send.at[h, idx], recv_sem=g_recv.at[h, src],
            device_id={"col": dst}, device_id_type=MESH)

    for h in range(H):
        panel_copy(h).wait()
        for dm in range(1, NCH):
            g_copy(h, c, (m + dm) % NCH * 2 + k, dm - 1).start()
        g_copy(h, c, sibling, NCH - 1).start()

    NA_CH = M // RB

    def pack(p, carry):
        for b in range(2):
            i = p * 2 + b

            @pl.when(i + 1 < NA_CH)
            def _():
                for cp in a_copies(i + 1, 1 - b):
                    cp.start()
            for cp in a_copies(i, b):
                cp.wait()
            rows = pl.ds(pl.multiple_of(i * RB, RB), RB)
            for q in range(CAP):
                AC[rows, q * BS:(q + 1) * BS] = abufs[b][ids[q]]
        return carry

    lax.fori_loop(0, NA_CH // 2, pack, 0)

    PARTS = ((1, KA, K - KA), (0, 0, KA))

    def e_copy(j, h, part, dev, d):
        p, first, count = part
        blk = E.at[j, pl.ds(first, count), pl.ds(h * wh, wh)]
        return pltpu.make_async_remote_copy(
            src_ref=blk, dst_ref=blk, send_sem=e_send.at[j, h, p, d], recv_sem=e_recv.at[j, h, p],
            device_id={"row": dev}, device_id_type=MESH)

    def flags(j, p):
        zs, xs = j // NX, j % NX
        along_z = (xs == x) | (p == 1)
        along_x = (zs == z) | (p == 0)
        return [along_z & (zs <= z) & (z + 1 < NZ), along_z & (zs >= z) & (z > 0),
                along_x & (xs <= x) & (x + 1 < NX), along_x & (xs >= x) & (x > 0)]

    def forward(j, h, part, act):
        for d in (2, 3, 0, 1):
            @pl.when(flags(j, part[0])[d])
            def _(d=d):
                act(e_copy(j, h, part, nbrs[d][1], d))

    def pair(bufs, sems, src, dst, i, j, dev):
        return [pltpu.make_async_remote_copy(
            src_ref=bufs[q].at[src], dst_ref=bufs[q + 2].at[dst], send_sem=sems[q].at[i], recv_sem=sems[q + 2].at[j],
            device_id={"col": dev}, device_id_type=MESH) for q in range(2)]

    def far_slot(j):
        return (j - (m + 1) * 2 * J + 2 * NR) % NR

    def half_copies(slot):
        return pair(half_bufs, half_sems, slot, slot, slot, slot, sibling)

    def mate_copies(jj):
        return pair(mate_bufs, mate_sems, jj, jj, jj, jj, sibling)

    def far_copies(j):
        slot, md = far_slot(j), j // (2 * J)
        at = ((m - md - 1 + NCH) % NCH, j % J, k)
        return pair(far_bufs, far_sems, slot, at, slot, at, j // J)

    def encode(value, dst, scales, slot, row0, i):
        top = jnp.maximum(jnp.max(jnp.abs(value), axis=0, keepdims=True), 1e-30)
        scales[slot, pl.ds(i, 1), :] = top * (1.0 / 32767.0)
        dst[slot, pl.ds(pl.multiple_of(row0, MB), MB), :] = jnp.round(value * (32767.0 / top)).astype(jnp.int16)

    def compute(j):
        jj, d = j % J, j // J
        far = d // 2 != m
        slot = far_slot(j)

        def rows_of(half, keep):
            def chunk(i, carry):
                row0 = half * HM + i * MM
                prod = jnp.dot(AC[pl.ds(pl.multiple_of(row0, MM), MM), :], E[j], preferred_element_type=jnp.float32)
                for o in range(J):
                    @pl.when(j == c * J + o)
                    def _(o=o):
                        out_ref[pl.ds(pl.multiple_of(row0, MM), MM), o * w:(o + 1) * w] = prod

                @pl.when(d == sibling)
                def _():
                    for u in range(MM // MB):
                        encode(prod[u * MB:(u + 1) * MB], mate_bufs[0], mate_bufs[1], jj, row0 + u * MB, row0 // MB + u)

                @pl.when(far)
                def _():
                    if keep:
                        Y[pl.ds(pl.multiple_of(i * MM, MM), MM), :] = prod
                    else:
                        for u in range(MM // MB):
                            encode(prod[u * MB:(u + 1) * MB], half_bufs[0], half_bufs[1], slot,
                                   i * MM + u * MB, i * (MM // MB) + u)
                return carry

            lax.fori_loop(0, HM // MM, chunk, 0)

        rows_of(1 - k, False)

        @pl.when(far)
        def _():
            for cp in half_copies(slot):
                cp.start()

        rows_of(k, True)

        @pl.when(d == sibling)
        def _():
            for cp in mate_copies(jj):
                cp.start()

        @pl.when(far)
        def _():
            for cp in half_copies(slot):
                cp.wait_recv()

            def chunk(i, carry):
                rows = pl.ds(pl.multiple_of(i * MB, MB), MB)
                value = Y[rows, :] + half_bufs[2][slot, rows, :].astype(jnp.float32) * half_bufs[3][slot, pl.ds(i, 1), :]
                encode(value, far_bufs[0], far_bufs[1], slot, i * MB, i)
                return carry

            lax.fori_loop(0, HM // MB, chunk, 0)
            for cp in far_copies(j):
                cp.start()

    for h in range(H):
        for dm in range(1, NCH):
            src = (m + dm) % NCH * 2 + k
            g_copy(h, src, sibling, 0).wait_recv()
            g_copy(h, src, sibling, NCH - 1 + dm).start()
        for dm in range(NCH):
            g_copy(h, (m + dm) % NCH * 2 + 1 - k, sibling, 0).wait_recv()
        for q in range(CAP):
            E[r, q * BS:(q + 1) * BS, h * wh:(h + 1) * wh] = G[h][pos[q]]
        for part in PARTS:
            forward(r, h, part, lambda cp: cp.start())
    compute(r)

    def zorder(i):
        near = jnp.minimum(z, NZ - 1 - z)
        t = (i + 1) // 2
        two = jnp.where(i % 2 == 1, z - t, z + t)
        one = jnp.where(z < NZ - 1 - z, z + (i - near), z - (i - near))
        return jnp.where(i <= 2 * near, two, one)

    def xorder(i):
        near = jnp.minimum(x, NX - 1 - x)
        t = (i + 1) // 2
        two = jnp.where(i % 2 == 1, x - t, x + t)
        one = jnp.where(x < NX - 1 - x, x + (i - near), x - (i - near))
        return jnp.where(i <= 2 * near, two, one)

    def step(s, carry):
        if NX == 2:
            last = s == 2 * NZ - 1
            d = jnp.where(last, 1, (s + 1) % 2)
            zi = jnp.where(last, NZ - 1, jnp.where(s % 2 == 1, (s + 1) // 2, s // 2 - 1))
            j = zorder(zi) * NX + jnp.where(d == 1, 1 - x, x)
        else:
            j = zorder(s // NX) * NX + xorder(s % NX)
        for h in range(H):
            for part in PARTS:
                e_copy(j, h, part, nbrs[0][1], 0).wait_recv()
                forward(j, h, part, lambda cp: cp.start())
        compute(j)
        return carry

    lax.fori_loop(1, NR, step, 0)

    for jj in range(J):
        for cp in mate_copies(jj):
            cp.wait_recv()
        for rel in range(NCH - 1):
            for half in range(2):
                for cp in pair(far_bufs, far_sems, 0, (rel, jj, half), 0, (rel, jj, half), sibling):
                    cp.wait_recv()

        def add(i, carry, jj=jj):
            rows = pl.ds(pl.multiple_of(i * MB, MB), MB)
            half, ih = i // (HM // MB), i % (HM // MB)
            inner = pl.ds(pl.multiple_of(ih * MB, MB), MB)
            total = out_ref[rows, jj * w:(jj + 1) * w]
            total += mate_bufs[2][jj, rows, :].astype(jnp.float32) * mate_bufs[3][jj, pl.ds(i, 1), :]
            for rel in range(NCH - 1):
                total += (far_bufs[2][rel, jj, half, inner, :].astype(jnp.float32)
                          * far_bufs[3][rel, jj, half, pl.ds(ih, 1), :])
            out_ref[rows, jj * w:(jj + 1) * w] = total
            return carry
        lax.fori_loop(0, M // MB, add, 0)

    for h in range(H):
        for idx in range(NC - 1):
            g_copy(h, c, sibling, idx).wait_send()

    def drain(j, carry):
        for h in range(H):
            for part in PARTS:
                forward(j, h, part, lambda cp: cp.wait_send())

        @pl.when(j // (2 * J) != m)
        def _():
            for cp in half_copies(far_slot(j)) + far_copies(j):
                cp.wait_send()
        return carry

    for jj in range(J):
        for cp in mate_copies(jj):
            cp.wait_send()
    lax.fori_loop(0, NR, drain, 0)


def body(NR, NC, anc_inv, panel, structure):
    c = lax.axis_index("col")
    r = lax.axis_index("row")
    M, cols = anc_inv.shape
    GB = cols // BS
    CAP = GB * 3 // 4 + 1
    PB, w = panel.shape[1] // BS, panel.shape[2]
    NX = 2
    while NX * NX * 2 < NR:
        NX *= 2
    NZ = NR // NX
    H = max(1, w // 128)
    wh = w // H
    J = NR // NC
    HM = M // 2
    MB = 256
    MM = min(512, HM)
    RB = 256
    K = CAP * BS
    KA = (CAP - (CAP + 3) // 6) * BS
    s = structure[0]
    n = s.shape[0]
    at = jnp.arange(n, dtype=jnp.int32)
    mine = s // GB == c
    rank = jnp.sum((at[None, :] < at[:, None]) & mine[None, :], axis=1)
    hot = mine[None, :] & (rank[None, :] == jnp.arange(CAP)[:, None])
    pos = n + jnp.sum(jnp.where(hot, at[None, :] - n, 0), axis=1).astype(jnp.int32)
    ids = jnp.sum(jnp.where(hot, (s - c * GB)[None, :], 0), axis=1).astype(jnp.int32)
    D = pltpu.SemaphoreType.DMA
    far = NR - 2 * J
    lead = (NC // 2 - 1, J, 2)

    def bufs(send, recv, rows):
        chunks = max(8, rows // MB)
        return [pltpu.VMEM((*send, rows, w), jnp.int16), pltpu.VMEM((*send, chunks, w), jnp.float32),
                pltpu.VMEM((*recv, rows, w), jnp.int16), pltpu.VMEM((*recv, chunks, w), jnp.float32)]

    def sems(send, recv):
        return [D(send), D(send), D(recv), D(recv)]

    smem = pl.BlockSpec(memory_space=pltpu.SMEM)
    hbm = pl.BlockSpec(memory_space=pl.ANY)
    total = pl.pallas_call(
        functools.partial(kernel, (NZ, NX, NC, CAP, H, MB, MM, KA)),
        out_shape=jax.ShapeDtypeStruct((M, J * w), jnp.float32),
        in_specs=[smem, smem, hbm, hbm],
        out_specs=pl.BlockSpec(memory_space=pltpu.VMEM),
        scratch_shapes=[
            [pltpu.VMEM((NC * PB + 1, BS, wh), jnp.bfloat16)] * H,
            pltpu.VMEM((NR, K, w), jnp.bfloat16),
            pltpu.VMEM((M, K), jnp.bfloat16),
            [pltpu.VMEM((GB, RB, BS), jnp.bfloat16)] * 2,
            pltpu.VMEM((HM, w), jnp.float32),
            bufs((far,), lead, HM), bufs((J,), (J,), M), bufs((far,), (far,), HM),
            D((H,)), D((2, GB)), D((H, NC - 1)), D((H, NC)), D((NR, H, 2, 4)), D((NR, H, 2)),
            sems((far,), lead), sems((J,), (J,)), sems((far,), (far,)),
        ],
        compiler_params=pltpu.CompilerParams(
            collective_id=0, has_side_effects=True, vmem_limit_bytes=63 * 2**20),
    )(ids, pos, anc_inv, panel.reshape(1, PB, BS, w))
    own_blocks = r * (M // BS) + jnp.arange(M // BS, dtype=jnp.int32)
    member = jnp.any(s[None, :] == own_blocks[:, None], axis=1)
    mask = jnp.repeat(member, BS)
    return jnp.where(mask[:, None], -total, 0.0)[None]


def solution(mesh):
    in_specs = (P("row", "col"), P(None, "col", "row"), P())
    out_specs = P(None, "row", "col")
    fn = functools.partial(body, mesh.shape["row"], mesh.shape["col"])
    return jax.shard_map(fn, mesh=mesh, in_specs=in_specs, out_specs=out_specs, check_vma=False)
```

```python
import functools

import jax
import jax.numpy as jnp
from jax import lax
from jax.experimental import pallas as pl
from jax.experimental.pallas import tpu as pltpu
from jax.sharding import PartitionSpec as P

BS = 128
MESH = pl.DeviceIdType.MESH


def kernel(dims, ids, pos, a_hbm, panel_hbm, out_ref,
           G, E, AC, abufs, Y, far_bufs, mate_bufs, half_bufs,
           l_sem, a_sem, g_send, g_recv, e_send, e_recv, far_sems, mate_sems, half_sems):
    NZ, NX, NC, CAP, H, MB, MM, KA = dims
    NR = NZ * NX
    J = NR // NC
    NCH = NC // 2
    r = lax.axis_index("row")
    c = lax.axis_index("col")
    z, x = r // NX, r % NX
    m, k = c // 2, c % 2
    sibling = m * 2 + 1 - k
    M, K = AC.shape
    HM = M // 2
    w = E.shape[2]
    wh = w // H
    PB = panel_hbm.shape[1]
    GB, RB = abufs[0].shape[:2]
    i32 = lambda v: v.astype(jnp.int32)
    nbrs = [(z + 1 < NZ, r + NX), (z > 0, r - NX), (x + 1 < NX, r + 1), (x > 0, r - 1)]

    def panel_copy(h):
        return pltpu.make_async_copy(
            panel_hbm.at[0, :, :, pl.ds(h * wh, wh)], G[h].at[pl.ds(c * PB, PB)], l_sem.at[h])

    def a_copies(i, b):
        rows = pl.ds(pl.multiple_of(i * RB, RB), RB)
        return [pltpu.make_async_copy(a_hbm.at[rows, pl.ds(q * BS, BS)], abufs[b].at[q], a_sem.at[b, q])
                for q in range(GB)]

    for h in range(H):
        panel_copy(h).start()
    for cp in a_copies(0, 0):
        cp.start()

    barrier = pltpu.get_barrier_semaphore()
    for dc in range(1, NC):
        pl.semaphore_signal(barrier, inc=1, device_id={"col": (c + dc) % NC}, device_id_type=MESH)
    for ok, dev in nbrs:
        @pl.when(ok)
        def _(dev=dev):
            pl.semaphore_signal(barrier, inc=1, device_id={"row": dev}, device_id_type=MESH)
    pl.semaphore_wait(barrier, NC - 1 + sum(i32(ok) for ok, _ in nbrs))

    for h in range(H):
        G[h][NC * PB] = jnp.zeros((BS, wh), jnp.bfloat16)

    def g_copy(h, src, dst, idx):
        blk = G[h].at[pl.ds(src * PB, PB)]
        return pltpu.make_async_remote_copy(
            src_ref=blk, dst_ref=blk, send_sem=g_send.at[h, idx], recv_sem=g_recv.at[h, src],
            device_id={"col": dst}, device_id_type=MESH)

    for h in range(H):
        panel_copy(h).wait()
        for dm in range(1, NCH):
            g_copy(h, c, (m + dm) % NCH * 2 + k, dm - 1).start()
        g_copy(h, c, sibling, NCH - 1).start()

    NA_CH = M // RB

    def pack(p, carry):
        for b in range(2):
            i = p * 2 + b

            @pl.when(i + 1 < NA_CH)
            def _():
                for cp in a_copies(i + 1, 1 - b):
                    cp.start()
            for cp in a_copies(i, b):
                cp.wait()
            rows = pl.ds(pl.multiple_of(i * RB, RB), RB)
            for q in range(CAP):
                AC[rows, q * BS:(q + 1) * BS] = abufs[b][ids[q]]
        return carry

    lax.fori_loop(0, NA_CH // 2, pack, 0)

    PARTS = ((1, KA, K - KA), (0, 0, KA))

    def e_copy(j, h, part, dev, d):
        p, first, count = part
        blk = E.at[j, pl.ds(first, count), pl.ds(h * wh, wh)]
        return pltpu.make_async_remote_copy(
            src_ref=blk, dst_ref=blk, send_sem=e_send.at[j, h, p, d], recv_sem=e_recv.at[j, h, p],
            device_id={"row": dev}, device_id_type=MESH)

    def flags(j, p):
        zs, xs = j // NX, j % NX
        along_z = (xs == x) | (p == 1)
        along_x = (zs == z) | (p == 0)
        return [along_z & (zs <= z) & (z + 1 < NZ), along_z & (zs >= z) & (z > 0),
                along_x & (xs <= x) & (x + 1 < NX), along_x & (xs >= x) & (x > 0)]

    def forward(j, h, part, act):
        for d in (2, 3, 0, 1):
            @pl.when(flags(j, part[0])[d])
            def _(d=d):
                act(e_copy(j, h, part, nbrs[d][1], d))

    def pair(bufs, sems, src, dst, i, j, dev, lo=0, n=None):
        lanes = (slice(None),) * (len(bufs[0].shape) - 1 - len(src)) + (pl.ds(lo, n or w),)
        return [pltpu.make_async_remote_copy(
            src_ref=bufs[q].at[(*src, *lanes)], dst_ref=bufs[q + 2].at[(*dst, *lanes)],
            send_sem=sems[q].at[i], recv_sem=sems[q + 2].at[j],
            device_id={"col": dev}, device_id_type=MESH) for q in range(2)]

    def far_slot(j):
        return (j - (m + 1) * 2 * J + 2 * NR) % NR

    def half_copies(slot, lo=0, n=None):
        return pair(half_bufs, half_sems, (slot,), (slot,), slot, (slot, int(lo > 0)), sibling, lo, n)

    def mate_copies(jj, lo=0, n=None):
        return pair(mate_bufs, mate_sems, (jj,), (jj,), jj, jj, sibling, lo, n)

    def far_copies(j, lo=0, n=None):
        slot, md = far_slot(j), j // (2 * J)
        at = ((m - md - 1 + NCH) % NCH, j % J, k)
        return pair(far_bufs, far_sems, (slot,), at, slot, at, j // J, lo, n)

    def encode(value, bufs, slot, i, lo, n):
        top = jnp.maximum(jnp.max(jnp.abs(value), axis=0, keepdims=True), 1e-30)
        bufs[1][*slot, i:i + 1, lo:lo + n] = top * (1.0 / 32767.0)
        bufs[0][*slot, i * MB:(i + 1) * MB, lo:lo + n] = jnp.round(
            value * (32767.0 / top)).astype(jnp.int16)

    def product(j, half, keep, lo, n):
        jj, d = j % J, j // J
        slot = far_slot(j)

        for i in range(HM // MM):
            rows = pl.ds(pl.multiple_of(half * HM + i * MM, MM), MM)
            prod = jnp.dot(AC[rows, :], E[j, :, lo:lo + n], preferred_element_type=jnp.float32)
            parts = [(i * (MM // MB) + u, prod[u * MB:(u + 1) * MB]) for u in range(MM // MB)]
            for o in range(J):
                @pl.when(j == c * J + o)
                def _(o=o):
                    out_ref[rows, o * w + lo:o * w + lo + n] = prod

            @pl.when(d == sibling)
            def _():
                for u, part in parts:
                    encode(part, mate_bufs, (jj, half), u, lo, n)

            @pl.when(d // 2 != m)
            def _():
                if keep:
                    Y[i * MM:(i + 1) * MM, lo:lo + n] = prod
                else:
                    for u, part in parts:
                        encode(part, half_bufs, (slot,), u, lo, n)

    def first_half(j, lo, n):
        product(j, 1 - k, False, lo, n)

        @pl.when(j // (2 * J) != m)
        def _():
            for cp in half_copies(far_slot(j), lo, n):
                cp.start()

    def second_half(j, lo, n):
        product(j, k, True, lo, n)
        slot = far_slot(j)

        @pl.when(j // J == sibling)
        def _():
            for cp in mate_copies(j % J, lo, n):
                cp.start()

        @pl.when(j // (2 * J) != m)
        def _():
            for cp in half_copies(slot, lo, n):
                cp.wait_recv()

            for i in range(HM // MB):
                rows = slice(i * MB, (i + 1) * MB)
                other = half_bufs[2][slot, rows, lo:lo + n].astype(jnp.float32)
                value = Y[rows, lo:lo + n] + other * half_bufs[3][slot, i:i + 1, lo:lo + n]
                encode(value, far_bufs, (slot,), i, lo, n)
            for cp in far_copies(j, lo, n):
                cp.start()

    for h in range(H):
        for dm in range(1, NCH):
            src = (m + dm) % NCH * 2 + k
            g_copy(h, src, sibling, 0).wait_recv()
            g_copy(h, src, sibling, NCH - 1 + dm).start()
        for dm in range(NCH):
            g_copy(h, (m + dm) % NCH * 2 + 1 - k, sibling, 0).wait_recv()
        for q in range(CAP):
            E[r, q * BS:(q + 1) * BS, h * wh:(h + 1) * wh] = G[h][pos[q]]
        for part in PARTS:
            forward(r, h, part, lambda cp: cp.start())

    def zorder(i):
        near = jnp.minimum(z, NZ - 1 - z)
        t = (i + 1) // 2
        two = jnp.where(i % 2 == 1, z - t, z + t)
        one = jnp.where(z < NZ - 1 - z, z + (i - near), z - (i - near))
        return jnp.where(i <= 2 * near, two, one)

    def xorder(i):
        near = jnp.minimum(x, NX - 1 - x)
        t = (i + 1) // 2
        two = jnp.where(i % 2 == 1, x - t, x + t)
        one = jnp.where(x < NX - 1 - x, x + (i - near), x - (i - near))
        return jnp.where(i <= 2 * near, two, one)

    def slice_at(s):
        if NX != 2:
            return zorder(s // NX) * NX + xorder(s % NX)
        lead = jnp.where((z > 0) & (z + 1 < NZ), min(2, NZ - 1), 1)
        u = s - lead - 1
        both = 2 * (NZ - 1 - lead)
        z_turn = (s <= lead) | ((u < both) & (u % 2 == 1))
        zi = jnp.where(s <= lead, s, jnp.where(u < both, jnp.where(u % 2 == 1, lead + 1 + u // 2, u // 2), u - both // 2))
        return zorder(zi) * NX + jnp.where(z_turn, x, 1 - x)

    def arrive(j, h):
        for part in PARTS:
            e_copy(j, h, part, nbrs[0][1], 0).wait_recv()
            forward(j, h, part, lambda cp: cp.start())

    def step(s, carry):
        j, before = slice_at(s), slice_at(s - 1)
        first_half(before, 0, w)
        for h in range(H):
            arrive(j, h)
            if h == 0:
                second_half(before, 0, w)
        return carry

    lax.fori_loop(1, NR - 1, step, 0)
    last, before = slice_at(jnp.int32(NR - 1)), slice_at(jnp.int32(NR - 2))
    first_half(before, 0, w)
    for h in range(H):
        arrive(last, h)
        if h == 0:
            second_half(before, 0, w)
        first_half(last, h * wh, wh)
        second_half(last, h * wh, wh)

    for jj in range(J):
        for cp in mate_copies(jj):
            cp.wait_recv()
        for rel in range(NCH - 1):
            for half in range(2):
                for cp in pair(far_bufs, far_sems, (0,), (rel, jj, half), 0, (rel, jj, half), sibling):
                    cp.wait_recv()

        def add(i, carry, jj=jj):
            rows = pl.ds(pl.multiple_of(i * MB, MB), MB)
            half, ih = i // (HM // MB), i % (HM // MB)
            inner = pl.ds(pl.multiple_of(ih * MB, MB), MB)
            total = out_ref[rows, jj * w:(jj + 1) * w]
            total += mate_bufs[2][jj, half, inner, :].astype(jnp.float32) * mate_bufs[3][jj, half, pl.ds(ih, 1), :]
            for rel in range(NCH - 1):
                total += (far_bufs[2][rel, jj, half, inner, :].astype(jnp.float32)
                          * far_bufs[3][rel, jj, half, pl.ds(ih, 1), :])
            out_ref[rows, jj * w:(jj + 1) * w] = total
            return carry
        lax.fori_loop(0, M // MB, add, 0)

    for h in range(H):
        for idx in range(NC - 1):
            g_copy(h, c, sibling, idx).wait_send()

    def drain(j, carry):
        for h in range(H):
            for part in PARTS:
                forward(j, h, part, lambda cp: cp.wait_send())

        @pl.when(j // (2 * J) != m)
        def _():
            for cp in half_copies(far_slot(j)) + far_copies(j):
                cp.wait_send()
        return carry

    for jj in range(J):
        for cp in mate_copies(jj):
            cp.wait_send()
    lax.fori_loop(0, NR, drain, 0)


def body(NR, NC, anc_inv, panel, structure):
    c = lax.axis_index("col")
    r = lax.axis_index("row")
    M, cols = anc_inv.shape
    GB = cols // BS
    CAP = GB * 3 // 4 + 1
    PB, w = panel.shape[1] // BS, panel.shape[2]
    NX = 2
    while NX * NX * 2 < NR:
        NX *= 2
    NZ = NR // NX
    H = max(1, w // 128)
    wh = w // H
    J = NR // NC
    HM = M // 2
    MB = 256
    MM = min(512, HM)
    RB = 256
    K = CAP * BS
    KA = (CAP - (CAP + 3) // 6) * BS
    s = structure[0]
    n = s.shape[0]
    at = jnp.arange(n, dtype=jnp.int32)
    mine = s // GB == c
    rank = jnp.sum((at[None, :] < at[:, None]) & mine[None, :], axis=1)
    hot = mine[None, :] & (rank[None, :] == jnp.arange(CAP)[:, None])
    pos = n + jnp.sum(jnp.where(hot, at[None, :] - n, 0), axis=1).astype(jnp.int32)
    ids = jnp.sum(jnp.where(hot, (s - c * GB)[None, :], 0), axis=1).astype(jnp.int32)
    D = pltpu.SemaphoreType.DMA
    far = NR - 2 * J
    lead = (NC // 2 - 1, J, 2)

    def bufs(send, recv, rows):
        chunks = max(8, rows // MB)
        return [pltpu.VMEM((*send, rows, w), jnp.int16), pltpu.VMEM((*send, chunks, w), jnp.float32),
                pltpu.VMEM((*recv, rows, w), jnp.int16), pltpu.VMEM((*recv, chunks, w), jnp.float32)]

    def sems(send, recv):
        return [D(send), D(send), D(recv), D(recv)]

    smem = pl.BlockSpec(memory_space=pltpu.SMEM)
    hbm = pl.BlockSpec(memory_space=pl.ANY)
    total = pl.pallas_call(
        functools.partial(kernel, (NZ, NX, NC, CAP, H, MB, MM, KA)),
        out_shape=jax.ShapeDtypeStruct((M, J * w), jnp.float32),
        in_specs=[smem, smem, hbm, hbm],
        out_specs=pl.BlockSpec(memory_space=pltpu.VMEM),
        scratch_shapes=[
            [pltpu.VMEM((NC * PB + 1, BS, wh), jnp.bfloat16)] * H,
            pltpu.VMEM((NR, K, w), jnp.bfloat16),
            pltpu.VMEM((M, K), jnp.bfloat16),
            [pltpu.VMEM((GB, RB, BS), jnp.bfloat16)] * 2,
            pltpu.VMEM((HM, w), jnp.float32),
            bufs((far,), lead, HM), bufs((J, 2), (J, 2), HM), bufs((far,), (far,), HM),
            D((H,)), D((2, GB)), D((H, NC - 1)), D((H, NC)), D((NR, H, 2, 4)), D((NR, H, 2)),
            sems((far,), lead), sems((J,), (J,)), sems((far,), (far, 2)),
        ],
        compiler_params=pltpu.CompilerParams(
            collective_id=0, has_side_effects=True, vmem_limit_bytes=63 * 2**20),
    )(ids, pos, anc_inv, panel.reshape(1, PB, BS, w))
    own_blocks = r * (M // BS) + jnp.arange(M // BS, dtype=jnp.int32)
    member = jnp.any(s[None, :] == own_blocks[:, None], axis=1)
    mask = jnp.repeat(member, BS)
    return jnp.where(mask[:, None], -total, 0.0)[None]


def solution(mesh):
    in_specs = (P("row", "col"), P(None, "col", "row"), P())
    out_specs = P(None, "row", "col")
    fn = functools.partial(body, mesh.shape["row"], mesh.shape["col"])
    return jax.shard_map(fn, mesh=mesh, in_specs=in_specs, out_specs=out_specs, check_vma=False)
```

```python
import functools

import jax
import jax.numpy as jnp
from jax import lax
from jax.experimental import pallas as pl
from jax.experimental.pallas import tpu as pltpu
from jax.sharding import PartitionSpec as P

BS = 128
MESH = pl.DeviceIdType.MESH


def kernel(dims, ids, pos, a_hbm, panel_hbm, out_ref,
           G, E, AC, abufs, Y, far_bufs, mate_bufs, half_bufs,
           l_sem, a_sem, g_send, g_recv, e_send, e_recv, far_sems, mate_sems, half_sems):
    NZ, NX, NC, CAP, H, MB, MM, KA = dims
    NR = NZ * NX
    J = NR // NC
    NCH = NC // 2
    r = lax.axis_index("row")
    c = lax.axis_index("col")
    z, x = r // NX, r % NX
    m, k = c // 2, c % 2
    sibling = m * 2 + 1 - k
    M, K = AC.shape
    HM = M // 2
    w = E.shape[2]
    wh = w // H
    PB = panel_hbm.shape[1]
    GB, RB = abufs[0].shape[:2]
    i32 = lambda v: v.astype(jnp.int32)
    nbrs = [(z + 1 < NZ, r + NX), (z > 0, r - NX), (x + 1 < NX, r + 1), (x > 0, r - 1)]

    def panel_copy(h):
        return pltpu.make_async_copy(
            panel_hbm.at[0, :, :, pl.ds(h * wh, wh)], G[h].at[pl.ds(c * PB, PB)], l_sem.at[h])

    def a_copies(i, b):
        rows = pl.ds(pl.multiple_of(i * RB, RB), RB)
        return [pltpu.make_async_copy(a_hbm.at[rows, pl.ds(q * BS, BS)], abufs[b].at[q], a_sem.at[b, q])
                for q in range(GB)]

    for h in range(H):
        panel_copy(h).start()
    for cp in a_copies(0, 0):
        cp.start()

    barrier = pltpu.get_barrier_semaphore()
    for dc in range(1, NC):
        pl.semaphore_signal(barrier, inc=1, device_id={"col": (c + dc) % NC}, device_id_type=MESH)
    for ok, dev in nbrs:
        @pl.when(ok)
        def _(dev=dev):
            pl.semaphore_signal(barrier, inc=1, device_id={"row": dev}, device_id_type=MESH)
    pl.semaphore_wait(barrier, NC - 1 + sum(i32(ok) for ok, _ in nbrs))

    for h in range(H):
        G[h][NC * PB] = jnp.zeros((BS, wh), jnp.bfloat16)

    def g_copy(h, src, dst, idx):
        blk = G[h].at[pl.ds(src * PB, PB)]
        return pltpu.make_async_remote_copy(
            src_ref=blk, dst_ref=blk, send_sem=g_send.at[h, idx], recv_sem=g_recv.at[h, src],
            device_id={"col": dst}, device_id_type=MESH)

    for h in range(H):
        panel_copy(h).wait()
        for dm in range(1, NCH):
            g_copy(h, c, (m + dm) % NCH * 2 + k, dm - 1).start()
        g_copy(h, c, sibling, NCH - 1).start()

    NA_CH = M // RB

    def pack(p, carry):
        for b in range(2):
            i = p * 2 + b

            @pl.when(i + 1 < NA_CH)
            def _():
                for cp in a_copies(i + 1, 1 - b):
                    cp.start()
            for cp in a_copies(i, b):
                cp.wait()
            rows = pl.ds(pl.multiple_of(i * RB, RB), RB)
            for q in range(CAP):
                AC[rows, q * BS:(q + 1) * BS] = abufs[b][ids[q]]
        return carry

    lax.fori_loop(0, NA_CH // 2, pack, 0)

    PARTS = ((1, KA, K - KA), (0, 0, KA))

    def e_copy(j, h, part, dev, d):
        p, first, count = part
        blk = E.at[j, pl.ds(first, count), pl.ds(h * wh, wh)]
        return pltpu.make_async_remote_copy(
            src_ref=blk, dst_ref=blk, send_sem=e_send.at[j, h, p, d], recv_sem=e_recv.at[j, h, p],
            device_id={"row": dev}, device_id_type=MESH)

    def flags(j, p):
        zs, xs = j // NX, j % NX
        along_z = (xs == x) | (p == 1)
        along_x = (zs == z) | (p == 0)
        return [along_z & (zs <= z) & (z + 1 < NZ), along_z & (zs >= z) & (z > 0),
                along_x & (xs <= x) & (x + 1 < NX), along_x & (xs >= x) & (x > 0)]

    def forward(j, h, part, act):
        for d in (2, 3, 0, 1):
            @pl.when(flags(j, part[0])[d])
            def _(d=d):
                act(e_copy(j, h, part, nbrs[d][1], d))

    def pair(bufs, sems, src, dst, i, j, dev, lo=0, n=None):
        lanes = (slice(None),) * (len(bufs[0].shape) - 1 - len(src)) + (pl.ds(lo, n or w),)
        return [pltpu.make_async_remote_copy(
            src_ref=bufs[q].at[(*src, *lanes)], dst_ref=bufs[q + 2].at[(*dst, *lanes)],
            send_sem=sems[q].at[i], recv_sem=sems[q + 2].at[j],
            device_id={"col": dev}, device_id_type=MESH) for q in range(2)]

    def far_slot(j):
        return (j - (m + 1) * 2 * J + 2 * NR) % NR

    def half_copies(slot, lo=0, n=None):
        return pair(half_bufs, half_sems, (slot,), (slot,), slot, (slot, int(lo > 0)), sibling, lo, n)

    def mate_copies(jj, lo=0, n=None):
        return pair(mate_bufs, mate_sems, (jj,), (jj,), jj, jj, sibling, lo, n)

    def far_copies(j, lo=0, n=None):
        slot, md = far_slot(j), j // (2 * J)
        at = ((m - md - 1 + NCH) % NCH, j % J, k)
        return pair(far_bufs, far_sems, (slot,), at, slot, at, j // J, lo, n)

    def encode(value, bufs, slot, i, lo, n):
        top = jnp.maximum(jnp.max(jnp.abs(value), axis=0, keepdims=True), 1e-30)
        bufs[1][*slot, i:i + 1, lo:lo + n] = top * (1.0 / 32767.0)
        bufs[0][*slot, i * MB:(i + 1) * MB, lo:lo + n] = jnp.round(
            value * (32767.0 / top)).astype(jnp.int16)

    def product(j, half, keep, lo, n):
        jj, d = j % J, j // J
        slot = far_slot(j)

        for i in range(HM // MM):
            rows = pl.ds(pl.multiple_of(half * HM + i * MM, MM), MM)
            prod = jnp.dot(AC[rows, :], E[j, :, lo:lo + n], preferred_element_type=jnp.float32)
            parts = [(i * (MM // MB) + u, prod[u * MB:(u + 1) * MB]) for u in range(MM // MB)]
            for o in range(J):
                @pl.when(j == c * J + o)
                def _(o=o):
                    out_ref[rows, o * w + lo:o * w + lo + n] = prod

            @pl.when(d == sibling)
            def _():
                for u, part in parts:
                    encode(part, mate_bufs, (jj, half), u, lo, n)

            @pl.when(d // 2 != m)
            def _():
                if keep:
                    Y[i * MM:(i + 1) * MM, lo:lo + n] = prod
                else:
                    for u, part in parts:
                        encode(part, half_bufs, (slot,), u, lo, n)

    def first_half(j, lo, n):
        product(j, 1 - k, False, lo, n)

        @pl.when(j // (2 * J) != m)
        def _():
            for cp in half_copies(far_slot(j), lo, n):
                cp.start()

    def second_half(j, lo, n):
        product(j, k, True, lo, n)
        slot = far_slot(j)

        @pl.when(j // J == sibling)
        def _():
            for cp in mate_copies(j % J, lo, n):
                cp.start()

        @pl.when(j // (2 * J) != m)
        def _():
            for cp in half_copies(slot, lo, n):
                cp.wait_recv()

            for i in range(HM // MB):
                rows = slice(i * MB, (i + 1) * MB)
                other = half_bufs[2][slot, rows, lo:lo + n].astype(jnp.float32)
                value = Y[rows, lo:lo + n] + other * half_bufs[3][slot, i:i + 1, lo:lo + n]
                encode(value, far_bufs, (slot,), i, lo, n)
            for cp in far_copies(j, lo, n):
                cp.start()

    for h in range(H):
        for dm in range(1, NCH):
            src = (m + dm) % NCH * 2 + k
            g_copy(h, src, sibling, 0).wait_recv()
            g_copy(h, src, sibling, NCH - 1 + dm).start()
        for dm in range(NCH):
            g_copy(h, (m + dm) % NCH * 2 + 1 - k, sibling, 0).wait_recv()
        for q in range(CAP):
            E[r, q * BS:(q + 1) * BS, h * wh:(h + 1) * wh] = G[h][pos[q]]
        for part in PARTS:
            forward(r, h, part, lambda cp: cp.start())

    def zorder(i):
        near = jnp.minimum(z, NZ - 1 - z)
        t = (i + 1) // 2
        two = jnp.where(i % 2 == 1, z - t, z + t)
        one = jnp.where(z < NZ - 1 - z, z + (i - near), z - (i - near))
        return jnp.where(i <= 2 * near, two, one)

    def xorder(i):
        near = jnp.minimum(x, NX - 1 - x)
        t = (i + 1) // 2
        two = jnp.where(i % 2 == 1, x - t, x + t)
        one = jnp.where(x < NX - 1 - x, x + (i - near), x - (i - near))
        return jnp.where(i <= 2 * near, two, one)

    lead = jnp.where((z > 0) & (z + 1 < NZ), min(2, NZ - 1), 1)

    def turn(s):
        u = s - lead - 1
        both = 2 * (NZ - 1 - lead)
        own = (s <= lead) | ((u < both) & (u % 2 == 1))
        zi = jnp.where(s <= lead, s, jnp.where(u < both, jnp.where(u % 2 == 1, lead + 1 + u // 2, u // 2), u - both // 2))
        return zi, own

    def slice_at(s):
        if NX != 2:
            return zorder(s // NX) * NX + xorder(s % NX)
        zi, own = turn(s)
        return zorder(zi) * NX + jnp.where(own, x, 1 - x)

    def pass_on(j, h, part):
        e_copy(j, h, part, nbrs[0][1], 0).wait_recv()
        forward(j, h, part, lambda cp: cp.start())

    def arrive(j, h):
        if NX != 2:
            pass_on(j, h, PARTS[0])
        else:
            @pl.when(j % NX == x)
            def _():
                pass_on(j, h, PARTS[0])
        pass_on(j, h, PARTS[1])

    def early(s):
        if NX == 2:
            zi, own = turn(s)
            first = NZ - 1 - lead
            end = jnp.where(own | (zi > first), zi, jnp.where(zi == first, NZ, zi + 1))

            def one(i, carry):
                for h in range(H):
                    pass_on(zorder(i) * NX + 1 - x, h, PARTS[0])
                return carry

            lax.fori_loop(zi, end, one, 0)

    def step(s, carry):
        j, before = slice_at(s), slice_at(s - 1)
        early(s)
        first_half(before, 0, w)
        for h in range(H):
            arrive(j, h)
            if h == 0:
                second_half(before, 0, w)
        return carry

    lax.fori_loop(1, NR - 1, step, 0)
    last, before = slice_at(jnp.int32(NR - 1)), slice_at(jnp.int32(NR - 2))
    first_half(before, 0, w)
    for h in range(H):
        arrive(last, h)
        if h == 0:
            second_half(before, 0, w)
        first_half(last, h * wh, wh)
        second_half(last, h * wh, wh)

    for jj in range(J):
        for cp in mate_copies(jj):
            cp.wait_recv()
        for rel in range(NCH - 1):
            for half in range(2):
                for cp in pair(far_bufs, far_sems, (0,), (rel, jj, half), 0, (rel, jj, half), sibling):
                    cp.wait_recv()

        def add(i, carry, jj=jj):
            rows = pl.ds(pl.multiple_of(i * MB, MB), MB)
            half, ih = i // (HM // MB), i % (HM // MB)
            inner = pl.ds(pl.multiple_of(ih * MB, MB), MB)
            total = out_ref[rows, jj * w:(jj + 1) * w]
            total += mate_bufs[2][jj, half, inner, :].astype(jnp.float32) * mate_bufs[3][jj, half, pl.ds(ih, 1), :]
            for rel in range(NCH - 1):
                total += (far_bufs[2][rel, jj, half, inner, :].astype(jnp.float32)
                          * far_bufs[3][rel, jj, half, pl.ds(ih, 1), :])
            out_ref[rows, jj * w:(jj + 1) * w] = total
            return carry
        lax.fori_loop(0, M // MB, add, 0)

    for h in range(H):
        for idx in range(NC - 1):
            g_copy(h, c, sibling, idx).wait_send()

    def drain(j, carry):
        for h in range(H):
            for part in PARTS:
                forward(j, h, part, lambda cp: cp.wait_send())

        @pl.when(j // (2 * J) != m)
        def _():
            for cp in half_copies(far_slot(j)) + far_copies(j):
                cp.wait_send()
        return carry

    for jj in range(J):
        for cp in mate_copies(jj):
            cp.wait_send()
    lax.fori_loop(0, NR, drain, 0)


def body(NR, NC, anc_inv, panel, structure):
    c = lax.axis_index("col")
    r = lax.axis_index("row")
    M, cols = anc_inv.shape
    GB = cols // BS
    CAP = GB * 3 // 4 + 1
    PB, w = panel.shape[1] // BS, panel.shape[2]
    NX = 2
    while NX * NX * 2 < NR:
        NX *= 2
    NZ = NR // NX
    H = max(1, w // 128)
    wh = w // H
    J = NR // NC
    HM = M // 2
    MB = 256
    MM = min(512, HM)
    RB = 256
    K = CAP * BS
    KA = (CAP - (CAP + 3) // 6) * BS
    s = structure[0]
    n = s.shape[0]
    at = jnp.arange(n, dtype=jnp.int32)
    mine = s // GB == c
    rank = jnp.sum((at[None, :] < at[:, None]) & mine[None, :], axis=1)
    hot = mine[None, :] & (rank[None, :] == jnp.arange(CAP)[:, None])
    pos = n + jnp.sum(jnp.where(hot, at[None, :] - n, 0), axis=1).astype(jnp.int32)
    ids = jnp.sum(jnp.where(hot, (s - c * GB)[None, :], 0), axis=1).astype(jnp.int32)
    D = pltpu.SemaphoreType.DMA
    far = NR - 2 * J
    lead = (NC // 2 - 1, J, 2)

    def bufs(send, recv, rows):
        chunks = max(8, rows // MB)
        return [pltpu.VMEM((*send, rows, w), jnp.int16), pltpu.VMEM((*send, chunks, w), jnp.float32),
                pltpu.VMEM((*recv, rows, w), jnp.int16), pltpu.VMEM((*recv, chunks, w), jnp.float32)]

    def sems(send, recv):
        return [D(send), D(send), D(recv), D(recv)]

    smem = pl.BlockSpec(memory_space=pltpu.SMEM)
    hbm = pl.BlockSpec(memory_space=pl.ANY)
    total = pl.pallas_call(
        functools.partial(kernel, (NZ, NX, NC, CAP, H, MB, MM, KA)),
        out_shape=jax.ShapeDtypeStruct((M, J * w), jnp.float32),
        in_specs=[smem, smem, hbm, hbm],
        out_specs=pl.BlockSpec(memory_space=pltpu.VMEM),
        scratch_shapes=[
            [pltpu.VMEM((NC * PB + 1, BS, wh), jnp.bfloat16)] * H,
            pltpu.VMEM((NR, K, w), jnp.bfloat16),
            pltpu.VMEM((M, K), jnp.bfloat16),
            [pltpu.VMEM((GB, RB, BS), jnp.bfloat16)] * 2,
            pltpu.VMEM((HM, w), jnp.float32),
            bufs((far,), lead, HM), bufs((J, 2), (J, 2), HM), bufs((far,), (far,), HM),
            D((H,)), D((2, GB)), D((H, NC - 1)), D((H, NC)), D((NR, H, 2, 4)), D((NR, H, 2)),
            sems((far,), lead), sems((J,), (J,)), sems((far,), (far, 2)),
        ],
        compiler_params=pltpu.CompilerParams(
            collective_id=0, has_side_effects=True, vmem_limit_bytes=63 * 2**20),
    )(ids, pos, anc_inv, panel.reshape(1, PB, BS, w))
    own_blocks = r * (M // BS) + jnp.arange(M // BS, dtype=jnp.int32)
    member = jnp.any(s[None, :] == own_blocks[:, None], axis=1)
    mask = jnp.repeat(member, BS)
    return jnp.where(mask[:, None], -total, 0.0)[None]


def solution(mesh):
    in_specs = (P("row", "col"), P(None, "col", "row"), P())
    out_specs = P(None, "row", "col")
    fn = functools.partial(body, mesh.shape["row"], mesh.shape["col"])
    return jax.shard_map(fn, mesh=mesh, in_specs=in_specs, out_specs=out_specs, check_vma=False)
```

```python
import functools

import jax
import jax.numpy as jnp
from jax import lax
from jax.experimental import pallas as pl
from jax.experimental.pallas import tpu as pltpu
from jax.sharding import PartitionSpec as P

BS = 128
MESH = pl.DeviceIdType.MESH


def kernel(dims, ids, pos, a_hbm, panel_hbm, out_ref,
           G, E, AC, abufs, Y, far_bufs, mate_bufs, half_bufs,
           l_sem, a_sem, g_send, g_recv, e_send, e_recv, far_sems, mate_sems, half_sems):
    NZ, NX, NC, CAP, H, MB, MM, KA = dims
    NR = NZ * NX
    J = NR // NC
    NCH = NC // 2
    r = lax.axis_index("row")
    c = lax.axis_index("col")
    z, x = r // NX, r % NX
    m, k = c // 2, c % 2
    sibling = m * 2 + 1 - k
    M, K = AC.shape
    HM = M // 2
    w = E.shape[2]
    wh = w // H
    PB = panel_hbm.shape[1]
    GB, RB = abufs[0].shape[:2]
    i32 = lambda v: v.astype(jnp.int32)
    nbrs = [(z + 1 < NZ, r + NX), (z > 0, r - NX), (x + 1 < NX, r + 1), (x > 0, r - 1)]

    def panel_copy(h):
        return pltpu.make_async_copy(
            panel_hbm.at[0, :, :, pl.ds(h * wh, wh)], G[h].at[pl.ds(c * PB, PB)], l_sem.at[h])

    def a_copies(i, b):
        rows = pl.ds(pl.multiple_of(i * RB, RB), RB)
        return [pltpu.make_async_copy(a_hbm.at[rows, pl.ds(q * BS, BS)], abufs[b].at[q], a_sem.at[b, q])
                for q in range(GB)]

    for h in range(H):
        panel_copy(h).start()
    for cp in a_copies(0, 0):
        cp.start()

    barrier = pltpu.get_barrier_semaphore()
    for dc in range(1, NC):
        pl.semaphore_signal(barrier, inc=1, device_id={"col": (c + dc) % NC}, device_id_type=MESH)
    for ok, dev in nbrs:
        @pl.when(ok)
        def _(dev=dev):
            pl.semaphore_signal(barrier, inc=1, device_id={"row": dev}, device_id_type=MESH)
    pl.semaphore_wait(barrier, NC - 1 + sum(i32(ok) for ok, _ in nbrs))

    for h in range(H):
        G[h][NC * PB] = jnp.zeros((BS, wh), jnp.bfloat16)

    def g_copy(h, src, dst, idx):
        blk = G[h].at[pl.ds(src * PB, PB)]
        return pltpu.make_async_remote_copy(
            src_ref=blk, dst_ref=blk, send_sem=g_send.at[h, idx], recv_sem=g_recv.at[h, src],
            device_id={"col": dst}, device_id_type=MESH)

    for h in range(H):
        panel_copy(h).wait()
        for dm in range(1, NCH):
            g_copy(h, c, (m + dm) % NCH * 2 + k, dm - 1).start()
        g_copy(h, c, sibling, NCH - 1).start()

    NA_CH = M // RB

    def pack(p, carry):
        for b in range(2):
            i = p * 2 + b

            @pl.when(i + 1 < NA_CH)
            def _():
                for cp in a_copies(i + 1, 1 - b):
                    cp.start()
            for cp in a_copies(i, b):
                cp.wait()
            rows = pl.ds(pl.multiple_of(i * RB, RB), RB)
            for q in range(CAP):
                AC[rows, q * BS:(q + 1) * BS] = abufs[b][ids[q]]
        return carry

    lax.fori_loop(0, NA_CH // 2, pack, 0)

    PARTS = ((0, 0, KA), (1, KA, K - KA))

    def e_copy(j, h, part, dev, d):
        p, first, count = part
        blk = E.at[j, pl.ds(first, count), pl.ds(h * wh, wh)]
        return pltpu.make_async_remote_copy(
            src_ref=blk, dst_ref=blk, send_sem=e_send.at[j, h, p, d], recv_sem=e_recv.at[j, h, p],
            device_id={"row": dev}, device_id_type=MESH)

    def flags(j, p):
        zs, xs = j // NX, j % NX
        along_z = (xs == x) | (p == 1)
        along_x = (zs == z) | (p == 0)
        return [along_z & (zs <= z) & (z + 1 < NZ), along_z & (zs >= z) & (z > 0),
                along_x & (xs <= x) & (x + 1 < NX), along_x & (xs >= x) & (x > 0)]

    def forward(j, h, part, act):
        for d in range(4):
            @pl.when(flags(j, part[0])[d])
            def _(d=d):
                act(e_copy(j, h, part, nbrs[d][1], d))

    def pair(bufs, sems, src, dst, i, j, dev, lo=0, n=None):
        lanes = (slice(None),) * (len(bufs[0].shape) - 1 - len(src)) + (pl.ds(lo, n or w),)
        return [pltpu.make_async_remote_copy(
            src_ref=bufs[q].at[(*src, *lanes)], dst_ref=bufs[q + 2].at[(*dst, *lanes)],
            send_sem=sems[q].at[i], recv_sem=sems[q + 2].at[j],
            device_id={"col": dev}, device_id_type=MESH) for q in range(2)]

    def far_slot(j):
        return (j - (m + 1) * 2 * J + 2 * NR) % NR

    def half_copies(slot, lo=0, n=None):
        return pair(half_bufs, half_sems, (slot,), (slot,), slot, (slot, int(lo > 0)), sibling, lo, n)

    def mate_copies(jj, lo=0, n=None):
        return pair(mate_bufs, mate_sems, (jj,), (jj,), jj, jj, sibling, lo, n)

    def far_copies(j, lo=0, n=None):
        slot, md = far_slot(j), j // (2 * J)
        at = ((m - md - 1 + NCH) % NCH, j % J, k)
        return pair(far_bufs, far_sems, (slot,), at, slot, at, j // J, lo, n)

    def encode(value, bufs, slot, i, lo, n):
        top = jnp.maximum(jnp.max(jnp.abs(value), axis=0, keepdims=True), 1e-30)
        bufs[1][*slot, i:i + 1, lo:lo + n] = top * (1.0 / 32767.0)
        bufs[0][*slot, i * MB:(i + 1) * MB, lo:lo + n] = jnp.round(
            value * (32767.0 / top)).astype(jnp.int16)

    def product(j, half, keep, lo, n):
        jj, d = j % J, j // J
        slot = far_slot(j)

        for i in range(HM // MM):
            rows = pl.ds(pl.multiple_of(half * HM + i * MM, MM), MM)
            prod = jnp.dot(AC[rows, :], E[j, :, lo:lo + n], preferred_element_type=jnp.float32)
            parts = [(i * (MM // MB) + u, prod[u * MB:(u + 1) * MB]) for u in range(MM // MB)]
            for o in range(J):
                @pl.when(j == c * J + o)
                def _(o=o):
                    out_ref[rows, o * w + lo:o * w + lo + n] = prod

            @pl.when(d == sibling)
            def _():
                for u, part in parts:
                    encode(part, mate_bufs, (jj, half), u, lo, n)

            @pl.when(d // 2 != m)
            def _():
                if keep:
                    Y[i * MM:(i + 1) * MM, lo:lo + n] = prod
                else:
                    for u, part in parts:
                        encode(part, half_bufs, (slot,), u, lo, n)

    def first_half(j, lo, n):
        product(j, 1 - k, False, lo, n)

        @pl.when(j // (2 * J) != m)
        def _():
            for cp in half_copies(far_slot(j), lo, n):
                cp.start()

    def second_half(j, lo, n):
        product(j, k, True, lo, n)
        slot = far_slot(j)

        @pl.when(j // J == sibling)
        def _():
            for cp in mate_copies(j % J, lo, n):
                cp.start()

        @pl.when(j // (2 * J) != m)
        def _():
            for cp in half_copies(slot, lo, n):
                cp.wait_recv()

            for i in range(HM // MB):
                rows = slice(i * MB, (i + 1) * MB)
                other = half_bufs[2][slot, rows, lo:lo + n].astype(jnp.float32)
                value = Y[rows, lo:lo + n] + other * half_bufs[3][slot, i:i + 1, lo:lo + n]
                encode(value, far_bufs, (slot,), i, lo, n)
            for cp in far_copies(j, lo, n):
                cp.start()

    for h in range(H):
        for dm in range(1, NCH):
            src = (m + dm) % NCH * 2 + k
            g_copy(h, src, sibling, 0).wait_recv()
            g_copy(h, src, sibling, NCH - 1 + dm).start()
        for dm in range(NCH):
            g_copy(h, (m + dm) % NCH * 2 + 1 - k, sibling, 0).wait_recv()
        for q in range(CAP):
            E[r, q * BS:(q + 1) * BS, h * wh:(h + 1) * wh] = G[h][pos[q]]
        for part in PARTS:
            forward(r, h, part, lambda cp: cp.start())

    def zorder(i):
        near = jnp.minimum(z, NZ - 1 - z)
        t = (i + 1) // 2
        two = jnp.where(i % 2 == 1, z - t, z + t)
        one = jnp.where(z < NZ - 1 - z, z + (i - near), z - (i - near))
        return jnp.where(i <= 2 * near, two, one)

    def xorder(i):
        near = jnp.minimum(x, NX - 1 - x)
        t = (i + 1) // 2
        two = jnp.where(i % 2 == 1, x - t, x + t)
        one = jnp.where(x < NX - 1 - x, x + (i - near), x - (i - near))
        return jnp.where(i <= 2 * near, two, one)

    def slice_at(s):
        if NX != 2:
            return zorder(s // NX) * NX + xorder(s % NX)
        lead = jnp.where((z > 0) & (z + 1 < NZ), min(2, NZ - 1), 1)
        u = s - lead - 1
        both = 2 * (NZ - 1 - lead)
        z_turn = (s <= lead) | ((u < both) & (u % 2 == 1))
        zi = jnp.where(s <= lead, s, jnp.where(u < both, jnp.where(u % 2 == 1, lead + 1 + u // 2, u // 2), u - both // 2))
        return zorder(zi) * NX + jnp.where(z_turn, x, 1 - x)

    def arrive(j, h):
        for part in PARTS:
            e_copy(j, h, part, nbrs[0][1], 0).wait_recv()
            forward(j, h, part, lambda cp: cp.start())

    def step(s, carry):
        j, before = slice_at(s), slice_at(s - 1)
        first_half(before, 0, w)
        for h in range(H):
            arrive(j, h)
            if h == 0:
                second_half(before, 0, w)
        return carry

    lax.fori_loop(1, NR - 1, step, 0)
    last, before = slice_at(jnp.int32(NR - 1)), slice_at(jnp.int32(NR - 2))
    first_half(before, 0, w)
    for h in range(H):
        arrive(last, h)
        if h == 0:
            second_half(before, 0, w)
        first_half(last, h * wh, wh)
        second_half(last, h * wh, wh)

    for jj in range(J):
        for cp in mate_copies(jj):
            cp.wait_recv()
        for rel in range(NCH - 1):
            for half in range(2):
                for cp in pair(far_bufs, far_sems, (0,), (rel, jj, half), 0, (rel, jj, half), sibling):
                    cp.wait_recv()

        def add(i, carry, jj=jj):
            rows = pl.ds(pl.multiple_of(i * MB, MB), MB)
            half, ih = i // (HM // MB), i % (HM // MB)
            inner = pl.ds(pl.multiple_of(ih * MB, MB), MB)
            total = out_ref[rows, jj * w:(jj + 1) * w]
            total += mate_bufs[2][jj, half, inner, :].astype(jnp.float32) * mate_bufs[3][jj, half, pl.ds(ih, 1), :]
            for rel in range(NCH - 1):
                total += (far_bufs[2][rel, jj, half, inner, :].astype(jnp.float32)
                          * far_bufs[3][rel, jj, half, pl.ds(ih, 1), :])
            out_ref[rows, jj * w:(jj + 1) * w] = total
            return carry
        lax.fori_loop(0, M // MB, add, 0)

    for h in range(H):
        for idx in range(NC - 1):
            g_copy(h, c, sibling, idx).wait_send()

    def drain(j, carry):
        for h in range(H):
            for part in PARTS:
                forward(j, h, part, lambda cp: cp.wait_send())

        @pl.when(j // (2 * J) != m)
        def _():
            for cp in half_copies(far_slot(j)) + far_copies(j):
                cp.wait_send()
        return carry

    for jj in range(J):
        for cp in mate_copies(jj):
            cp.wait_send()
    lax.fori_loop(0, NR, drain, 0)


def body(NR, NC, anc_inv, panel, structure):
    c = lax.axis_index("col")
    r = lax.axis_index("row")
    M, cols = anc_inv.shape
    GB = cols // BS
    CAP = GB * 3 // 4 + 1
    PB, w = panel.shape[1] // BS, panel.shape[2]
    NX = 2
    while NX * NX * 2 < NR:
        NX *= 2
    NZ = NR // NX
    H = max(1, w // 128)
    wh = w // H
    J = NR // NC
    HM = M // 2
    MB = 256
    MM = min(512, HM)
    RB = 256
    K = CAP * BS
    KA = (CAP - (CAP + 7) // 10) * BS
    s = structure[0]
    n = s.shape[0]
    at = jnp.arange(n, dtype=jnp.int32)
    mine = s // GB == c
    rank = jnp.sum((at[None, :] < at[:, None]) & mine[None, :], axis=1)
    hot = mine[None, :] & (rank[None, :] == jnp.arange(CAP)[:, None])
    pos = n + jnp.sum(jnp.where(hot, at[None, :] - n, 0), axis=1).astype(jnp.int32)
    ids = jnp.sum(jnp.where(hot, (s - c * GB)[None, :], 0), axis=1).astype(jnp.int32)
    D = pltpu.SemaphoreType.DMA
    far = NR - 2 * J
    lead = (NC // 2 - 1, J, 2)

    def bufs(send, recv, rows):
        chunks = max(8, rows // MB)
        return [pltpu.VMEM((*send, rows, w), jnp.int16), pltpu.VMEM((*send, chunks, w), jnp.float32),
                pltpu.VMEM((*recv, rows, w), jnp.int16), pltpu.VMEM((*recv, chunks, w), jnp.float32)]

    def sems(send, recv):
        return [D(send), D(send), D(recv), D(recv)]

    smem = pl.BlockSpec(memory_space=pltpu.SMEM)
    hbm = pl.BlockSpec(memory_space=pl.ANY)
    total = pl.pallas_call(
        functools.partial(kernel, (NZ, NX, NC, CAP, H, MB, MM, KA)),
        out_shape=jax.ShapeDtypeStruct((M, J * w), jnp.float32),
        in_specs=[smem, smem, hbm, hbm],
        out_specs=pl.BlockSpec(memory_space=pltpu.VMEM),
        scratch_shapes=[
            [pltpu.VMEM((NC * PB + 1, BS, wh), jnp.bfloat16)] * H,
            pltpu.VMEM((NR, K, w), jnp.bfloat16),
            pltpu.VMEM((M, K), jnp.bfloat16),
            [pltpu.VMEM((GB, RB, BS), jnp.bfloat16)] * 2,
            pltpu.VMEM((HM, w), jnp.float32),
            bufs((far,), lead, HM), bufs((J, 2), (J, 2), HM), bufs((far,), (far,), HM),
            D((H,)), D((2, GB)), D((H, NC - 1)), D((H, NC)), D((NR, H, 2, 4)), D((NR, H, 2)),
            sems((far,), lead), sems((J,), (J,)), sems((far,), (far, 2)),
        ],
        compiler_params=pltpu.CompilerParams(
            collective_id=0, has_side_effects=True, vmem_limit_bytes=63 * 2**20),
    )(ids, pos, anc_inv, panel.reshape(1, PB, BS, w))
    own_blocks = r * (M // BS) + jnp.arange(M // BS, dtype=jnp.int32)
    member = jnp.any(s[None, :] == own_blocks[:, None], axis=1)
    mask = jnp.repeat(member, BS)
    return jnp.where(mask[:, None], -total, 0.0)[None]


def solution(mesh):
    in_specs = (P("row", "col"), P(None, "col", "row"), P())
    out_specs = P(None, "row", "col")
    fn = functools.partial(body, mesh.shape["row"], mesh.shape["col"])
    return jax.shard_map(fn, mesh=mesh, in_specs=in_specs, out_specs=out_specs, check_vma=False)
```

```python
import functools

import jax
import jax.numpy as jnp
from jax import lax
from jax.experimental import pallas as pl
from jax.experimental.pallas import tpu as pltpu
from jax.sharding import PartitionSpec as P

BS = 128
MESH = pl.DeviceIdType.MESH


def kernel(dims, ids, pos, a_hbm, panel_hbm, out_ref,
           G, E, AC, abufs, Y, far_bufs, mate_bufs, half_bufs,
           l_sem, a_sem, g_send, g_recv, e_send, e_recv, far_sems, mate_sems, half_sems):
    NZ, NX, NC, CAP, H, MB, MM, KA = dims
    NR = NZ * NX
    J = NR // NC
    NCH = NC // 2
    r = lax.axis_index("row")
    c = lax.axis_index("col")
    z, x = r // NX, r % NX
    m, k = c // 2, c % 2
    sibling = m * 2 + 1 - k
    M, K = AC.shape
    HM = M // 2
    w = E.shape[2]
    wh = w // H
    PB = panel_hbm.shape[1]
    GB, RB = abufs[0].shape[:2]
    i32 = lambda v: v.astype(jnp.int32)
    nbrs = [(z + 1 < NZ, r + NX), (z > 0, r - NX), (x + 1 < NX, r + 1), (x > 0, r - 1)]

    def panel_copy(h):
        return pltpu.make_async_copy(
            panel_hbm.at[0, :, :, pl.ds(h * wh, wh)], G[h].at[pl.ds(c * PB, PB)], l_sem.at[h])

    def a_copies(i, b):
        rows = pl.ds(pl.multiple_of(i * RB, RB), RB)
        return [pltpu.make_async_copy(a_hbm.at[rows, pl.ds(q * BS, BS)], abufs[b].at[q], a_sem.at[b, q])
                for q in range(GB)]

    for h in range(H):
        panel_copy(h).start()
    for cp in a_copies(0, 0):
        cp.start()

    barrier = pltpu.get_barrier_semaphore()
    for dc in range(1, NC):
        pl.semaphore_signal(barrier, inc=1, device_id={"col": (c + dc) % NC}, device_id_type=MESH)
    for ok, dev in nbrs:
        @pl.when(ok)
        def _(dev=dev):
            pl.semaphore_signal(barrier, inc=1, device_id={"row": dev}, device_id_type=MESH)
    pl.semaphore_wait(barrier, NC - 1 + sum(i32(ok) for ok, _ in nbrs))

    for h in range(H):
        G[h][NC * PB] = jnp.zeros((BS, wh), jnp.bfloat16)

    def g_copy(h, src, dst, idx):
        blk = G[h].at[pl.ds(src * PB, PB)]
        return pltpu.make_async_remote_copy(
            src_ref=blk, dst_ref=blk, send_sem=g_send.at[h, idx], recv_sem=g_recv.at[h, src],
            device_id={"col": dst}, device_id_type=MESH)

    for h in range(H):
        panel_copy(h).wait()
        for dm in range(1, NCH):
            g_copy(h, c, (m + dm) % NCH * 2 + k, dm - 1).start()
        g_copy(h, c, sibling, NCH - 1).start()

    NA_CH = M // RB

    def pack(p, carry):
        for b in range(2):
            i = p * 2 + b

            @pl.when(i + 1 < NA_CH)
            def _():
                for cp in a_copies(i + 1, 1 - b):
                    cp.start()
            for cp in a_copies(i, b):
                cp.wait()
            rows = pl.ds(pl.multiple_of(i * RB, RB), RB)
            for q in range(CAP):
                AC[rows, q * BS:(q + 1) * BS] = abufs[b][ids[q]]
        return carry

    lax.fori_loop(0, NA_CH // 2, pack, 0)

    PARTS = ((0, 0, KA), (1, KA, K - KA))

    def e_copy(j, h, part, dev, d):
        p, first, count = part
        blk = E.at[j, pl.ds(first, count), pl.ds(h * wh, wh)]
        return pltpu.make_async_remote_copy(
            src_ref=blk, dst_ref=blk, send_sem=e_send.at[j, h, p, d], recv_sem=e_recv.at[j, h, p],
            device_id={"row": dev}, device_id_type=MESH)

    def flags(j, p):
        zs, xs = j // NX, j % NX
        along_z = (xs == x) | (p == 1)
        along_x = (zs == z) | (p == 0)
        return [along_z & (zs <= z) & (z + 1 < NZ), along_z & (zs >= z) & (z > 0),
                along_x & (xs <= x) & (x + 1 < NX), along_x & (xs >= x) & (x > 0)]

    def forward(j, h, part, act, ways=range(4)):
        for d in ways:
            @pl.when(flags(j, part[0])[d])
            def _(d=d):
                act(e_copy(j, h, part, nbrs[d][1], d))

    def pair(bufs, sems, src, dst, i, j, dev, lo=0, n=None):
        lanes = (slice(None),) * (len(bufs[0].shape) - 1 - len(src)) + (pl.ds(lo, n or w),)
        return [pltpu.make_async_remote_copy(
            src_ref=bufs[q].at[(*src, *lanes)], dst_ref=bufs[q + 2].at[(*dst, *lanes)],
            send_sem=sems[q].at[i], recv_sem=sems[q + 2].at[j],
            device_id={"col": dev}, device_id_type=MESH) for q in range(2)]

    def far_slot(j):
        return (j - (m + 1) * 2 * J + 2 * NR) % NR

    def half_copies(slot, lo=0, n=None):
        return pair(half_bufs, half_sems, (slot,), (slot,), slot, (slot, int(lo > 0)), sibling, lo, n)

    def mate_copies(jj, lo=0, n=None):
        return pair(mate_bufs, mate_sems, (jj,), (jj,), jj, jj, sibling, lo, n)

    def far_copies(j, lo=0, n=None):
        slot, md = far_slot(j), j // (2 * J)
        at = ((m - md - 1 + NCH) % NCH, j % J, k)
        return pair(far_bufs, far_sems, (slot,), at, slot, at, j // J, lo, n)

    def encode(value, bufs, slot, i, lo, n):
        top = jnp.maximum(jnp.max(jnp.abs(value), axis=0, keepdims=True), 1e-30)
        bufs[1][*slot, i:i + 1, lo:lo + n] = top * (1.0 / 32767.0)
        bufs[0][*slot, i * MB:(i + 1) * MB, lo:lo + n] = jnp.round(
            value * (32767.0 / top)).astype(jnp.int16)

    def product(j, half, keep, lo, n):
        jj, d = j % J, j // J
        slot = far_slot(j)

        for i in range(HM // MM):
            rows = pl.ds(pl.multiple_of(half * HM + i * MM, MM), MM)
            prod = jnp.dot(AC[rows, :], E[j, :, lo:lo + n], preferred_element_type=jnp.float32)
            parts = [(i * (MM // MB) + u, prod[u * MB:(u + 1) * MB]) for u in range(MM // MB)]
            for o in range(J):
                @pl.when(j == c * J + o)
                def _(o=o):
                    out_ref[rows, o * w + lo:o * w + lo + n] = prod

            @pl.when(d == sibling)
            def _():
                for u, part in parts:
                    encode(part, mate_bufs, (jj, half), u, lo, n)

            @pl.when(d // 2 != m)
            def _():
                if keep:
                    Y[i * MM:(i + 1) * MM, lo:lo + n] = prod
                else:
                    for u, part in parts:
                        encode(part, half_bufs, (slot,), u, lo, n)

    def first_half(j, lo, n):
        product(j, 1 - k, False, lo, n)

        @pl.when(j // (2 * J) != m)
        def _():
            for cp in half_copies(far_slot(j), lo, n):
                cp.start()

    def second_half(j, lo, n):
        product(j, k, True, lo, n)
        slot = far_slot(j)

        @pl.when(j // J == sibling)
        def _():
            for cp in mate_copies(j % J, lo, n):
                cp.start()

        @pl.when(j // (2 * J) != m)
        def _():
            for cp in half_copies(slot, lo, n):
                cp.wait_recv()

            for i in range(HM // MB):
                rows = slice(i * MB, (i + 1) * MB)
                other = half_bufs[2][slot, rows, lo:lo + n].astype(jnp.float32)
                value = Y[rows, lo:lo + n] + other * half_bufs[3][slot, i:i + 1, lo:lo + n]
                encode(value, far_bufs, (slot,), i, lo, n)
            for cp in far_copies(j, lo, n):
                cp.start()

    for h in range(H):
        for dm in range(1, NCH):
            src = (m + dm) % NCH * 2 + k
            g_copy(h, src, sibling, 0).wait_recv()
            g_copy(h, src, sibling, NCH - 1 + dm).start()
        for dm in range(NCH):
            g_copy(h, (m + dm) % NCH * 2 + 1 - k, sibling, 0).wait_recv()
        for q in range(CAP):
            E[r, q * BS:(q + 1) * BS, h * wh:(h + 1) * wh] = G[h][pos[q]]
        for part in PARTS:
            forward(r, h, part, lambda cp: cp.start())

    def zorder(i):
        near = jnp.minimum(z, NZ - 1 - z)
        t = (i + 1) // 2
        two = jnp.where(i % 2 == 1, z - t, z + t)
        one = jnp.where(z < NZ - 1 - z, z + (i - near), z - (i - near))
        return jnp.where(i <= 2 * near, two, one)

    def xorder(i):
        near = jnp.minimum(x, NX - 1 - x)
        t = (i + 1) // 2
        two = jnp.where(i % 2 == 1, x - t, x + t)
        one = jnp.where(x < NX - 1 - x, x + (i - near), x - (i - near))
        return jnp.where(i <= 2 * near, two, one)

    lead = jnp.where((z > 0) & (z + 1 < NZ), min(2, NZ - 1), 1)

    def turn(s):
        u = s - lead - 1
        both = 2 * (NZ - 1 - lead)
        own = (s <= lead) | ((u < both) & (u % 2 == 1))
        zi = jnp.where(s <= lead, s, jnp.where(u < both, jnp.where(u % 2 == 1, lead + 1 + u // 2, u // 2), u - both // 2))
        return zi, own

    def slice_at(s):
        if NX != 2:
            return zorder(s // NX) * NX + xorder(s % NX)
        zi, own = turn(s)
        return zorder(zi) * NX + jnp.where(own, x, 1 - x)

    def start(cp):
        cp.start()

    def arrive(s, h):
        j = slice_at(s)
        for part in PARTS:
            e_copy(j, h, part, nbrs[0][1], 0).wait_recv()
            if NX != 2:
                forward(j, h, part, start)
                continue
            forward(j, h, part, start, (0, 1))
            if part[0] == 0:
                zi, own = turn(s)

                @pl.when(jnp.logical_not(own) & (zi + 1 < NZ))
                def _():
                    forward(zorder(zi + 1) * NX + x, h, part, start, (2, 3))

    def step(s, carry):
        before = slice_at(s - 1)
        first_half(before, 0, w)
        for h in range(H):
            arrive(s, h)
            if h == 0:
                second_half(before, 0, w)
        return carry

    lax.fori_loop(1, NR - 1, step, 0)
    end = jnp.int32(NR - 1)
    last, before = slice_at(end), slice_at(end - 1)
    first_half(before, 0, w)
    for h in range(H):
        arrive(end, h)
        if h == 0:
            second_half(before, 0, w)
        first_half(last, h * wh, wh)
        second_half(last, h * wh, wh)

    for jj in range(J):
        for cp in mate_copies(jj):
            cp.wait_recv()
        for rel in range(NCH - 1):
            for half in range(2):
                for cp in pair(far_bufs, far_sems, (0,), (rel, jj, half), 0, (rel, jj, half), sibling):
                    cp.wait_recv()

        def add(i, carry, jj=jj):
            rows = pl.ds(pl.multiple_of(i * MB, MB), MB)
            half, ih = i // (HM // MB), i % (HM // MB)
            inner = pl.ds(pl.multiple_of(ih * MB, MB), MB)
            total = out_ref[rows, jj * w:(jj + 1) * w]
            total += mate_bufs[2][jj, half, inner, :].astype(jnp.float32) * mate_bufs[3][jj, half, pl.ds(ih, 1), :]
            for rel in range(NCH - 1):
                total += (far_bufs[2][rel, jj, half, inner, :].astype(jnp.float32)
                          * far_bufs[3][rel, jj, half, pl.ds(ih, 1), :])
            out_ref[rows, jj * w:(jj + 1) * w] = total
            return carry
        lax.fori_loop(0, M // MB, add, 0)

    for h in range(H):
        for idx in range(NC - 1):
            g_copy(h, c, sibling, idx).wait_send()

    def drain(j, carry):
        for h in range(H):
            for part in PARTS:
                forward(j, h, part, lambda cp: cp.wait_send())

        @pl.when(j // (2 * J) != m)
        def _():
            for cp in half_copies(far_slot(j)) + far_copies(j):
                cp.wait_send()
        return carry

    for jj in range(J):
        for cp in mate_copies(jj):
            cp.wait_send()
    lax.fori_loop(0, NR, drain, 0)


def body(NR, NC, anc_inv, panel, structure):
    c = lax.axis_index("col")
    r = lax.axis_index("row")
    M, cols = anc_inv.shape
    GB = cols // BS
    CAP = GB * 3 // 4 + 1
    PB, w = panel.shape[1] // BS, panel.shape[2]
    NX = 2
    while NX * NX * 2 < NR:
        NX *= 2
    NZ = NR // NX
    H = max(1, w // 128)
    wh = w // H
    J = NR // NC
    HM = M // 2
    MB = 256
    MM = min(512, HM)
    RB = 256
    K = CAP * BS
    KA = (CAP - (CAP + 7) // 10) * BS
    s = structure[0]
    n = s.shape[0]
    at = jnp.arange(n, dtype=jnp.int32)
    mine = s // GB == c
    rank = jnp.sum((at[None, :] < at[:, None]) & mine[None, :], axis=1)
    hot = mine[None, :] & (rank[None, :] == jnp.arange(CAP)[:, None])
    pos = n + jnp.sum(jnp.where(hot, at[None, :] - n, 0), axis=1).astype(jnp.int32)
    ids = jnp.sum(jnp.where(hot, (s - c * GB)[None, :], 0), axis=1).astype(jnp.int32)
    D = pltpu.SemaphoreType.DMA
    far = NR - 2 * J
    lead = (NC // 2 - 1, J, 2)

    def bufs(send, recv, rows):
        chunks = max(8, rows // MB)
        return [pltpu.VMEM((*send, rows, w), jnp.int16), pltpu.VMEM((*send, chunks, w), jnp.float32),
                pltpu.VMEM((*recv, rows, w), jnp.int16), pltpu.VMEM((*recv, chunks, w), jnp.float32)]

    def sems(send, recv):
        return [D(send), D(send), D(recv), D(recv)]

    smem = pl.BlockSpec(memory_space=pltpu.SMEM)
    hbm = pl.BlockSpec(memory_space=pl.ANY)
    total = pl.pallas_call(
        functools.partial(kernel, (NZ, NX, NC, CAP, H, MB, MM, KA)),
        out_shape=jax.ShapeDtypeStruct((M, J * w), jnp.float32),
        in_specs=[smem, smem, hbm, hbm],
        out_specs=pl.BlockSpec(memory_space=pltpu.VMEM),
        scratch_shapes=[
            [pltpu.VMEM((NC * PB + 1, BS, wh), jnp.bfloat16)] * H,
            pltpu.VMEM((NR, K, w), jnp.bfloat16),
            pltpu.VMEM((M, K), jnp.bfloat16),
            [pltpu.VMEM((GB, RB, BS), jnp.bfloat16)] * 2,
            pltpu.VMEM((HM, w), jnp.float32),
            bufs((far,), lead, HM), bufs((J, 2), (J, 2), HM), bufs((far,), (far,), HM),
            D((H,)), D((2, GB)), D((H, NC - 1)), D((H, NC)), D((NR, H, 2, 4)), D((NR, H, 2)),
            sems((far,), lead), sems((J,), (J,)), sems((far,), (far, 2)),
        ],
        compiler_params=pltpu.CompilerParams(
            collective_id=0, has_side_effects=True, vmem_limit_bytes=63 * 2**20),
    )(ids, pos, anc_inv, panel.reshape(1, PB, BS, w))
    own_blocks = r * (M // BS) + jnp.arange(M // BS, dtype=jnp.int32)
    member = jnp.any(s[None, :] == own_blocks[:, None], axis=1)
    mask = jnp.repeat(member, BS)
    return jnp.where(mask[:, None], -total, 0.0)[None]


def solution(mesh):
    in_specs = (P("row", "col"), P(None, "col", "row"), P())
    out_specs = P(None, "row", "col")
    fn = functools.partial(body, mesh.shape["row"], mesh.shape["col"])
    return jax.shard_map(fn, mesh=mesh, in_specs=in_specs, out_specs=out_specs, check_vma=False)
```

```python
import functools

import jax
import jax.numpy as jnp
from jax import lax
from jax.experimental import pallas as pl
from jax.experimental.pallas import tpu as pltpu
from jax.sharding import PartitionSpec as P

BS = 128
MESH = pl.DeviceIdType.MESH


def kernel(dims, ids, pos, a_hbm, panel_hbm, out_ref,
           G, E, AC, abufs, Y, far_bufs, mate_bufs, half_bufs,
           l_sem, a_sem, g_send, g_recv, e_send, e_recv, far_sems, mate_sems, half_sems):
    NZ, NX, NC, CAP, H, MB, MM, KA = dims
    NR = NZ * NX
    J = NR // NC
    NCH = NC // 2
    r = lax.axis_index("row")
    c = lax.axis_index("col")
    z, x = r // NX, r % NX
    m, k = c // 2, c % 2
    sibling = m * 2 + 1 - k
    M, K = AC.shape
    HM = M // 2
    w = E.shape[2]
    wh = w // H
    PB = panel_hbm.shape[1]
    GB, RB = abufs[0].shape[:2]
    i32 = lambda v: v.astype(jnp.int32)
    nbrs = [(z + 1 < NZ, r + NX), (z > 0, r - NX), (x + 1 < NX, r + 1), (x > 0, r - 1)]

    def panel_copy(h):
        return pltpu.make_async_copy(
            panel_hbm.at[0, :, :, pl.ds(h * wh, wh)], G[h].at[pl.ds(c * PB, PB)], l_sem.at[h])

    def a_copies(i, b):
        rows = pl.ds(pl.multiple_of(i * RB, RB), RB)
        return [pltpu.make_async_copy(a_hbm.at[rows, pl.ds(q * BS, BS)], abufs[b].at[q], a_sem.at[b, q])
                for q in range(GB)]

    for h in range(H):
        panel_copy(h).start()
    for cp in a_copies(0, 0):
        cp.start()

    barrier = pltpu.get_barrier_semaphore()
    for dc in range(1, NC):
        pl.semaphore_signal(barrier, inc=1, device_id={"col": (c + dc) % NC}, device_id_type=MESH)
    for ok, dev in nbrs:
        @pl.when(ok)
        def _(dev=dev):
            pl.semaphore_signal(barrier, inc=1, device_id={"row": dev}, device_id_type=MESH)
    pl.semaphore_wait(barrier, NC - 1 + sum(i32(ok) for ok, _ in nbrs))

    for h in range(H):
        G[h][NC * PB] = jnp.zeros((BS, wh), jnp.bfloat16)

    def g_copy(h, src, dst, idx):
        blk = G[h].at[pl.ds(src * PB, PB)]
        return pltpu.make_async_remote_copy(
            src_ref=blk, dst_ref=blk, send_sem=g_send.at[h, idx], recv_sem=g_recv.at[h, src],
            device_id={"col": dst}, device_id_type=MESH)

    for h in range(H):
        panel_copy(h).wait()
        for dm in range(1, NCH):
            g_copy(h, c, (m + dm) % NCH * 2 + k, dm - 1).start()
        g_copy(h, c, sibling, NCH - 1).start()

    NA_CH = M // RB

    def pack(p, carry):
        for b in range(2):
            i = p * 2 + b

            @pl.when(i + 1 < NA_CH)
            def _():
                for cp in a_copies(i + 1, 1 - b):
                    cp.start()
            for cp in a_copies(i, b):
                cp.wait()
            rows = pl.ds(pl.multiple_of(i * RB, RB), RB)
            for q in range(CAP):
                AC[rows, q * BS:(q + 1) * BS] = abufs[b][ids[q]]
        return carry

    lax.fori_loop(0, NA_CH // 2, pack, 0)

    PARTS = ((1, KA, K - KA), (0, 0, KA))

    def e_copy(j, h, part, dev, d):
        p, first, count = part
        blk = E.at[j, pl.ds(first, count), pl.ds(h * wh, wh)]
        return pltpu.make_async_remote_copy(
            src_ref=blk, dst_ref=blk, send_sem=e_send.at[j, h, p, d], recv_sem=e_recv.at[j, h, p],
            device_id={"row": dev}, device_id_type=MESH)

    def flags(j, p):
        zs, xs = j // NX, j % NX
        along_z = (xs == x) | (p == 1)
        along_x = (zs == z) | (p == 0)
        return [along_z & (zs <= z) & (z + 1 < NZ), along_z & (zs >= z) & (z > 0),
                along_x & (xs <= x) & (x + 1 < NX), along_x & (xs >= x) & (x > 0)]

    def forward(j, h, part, act):
        for d in range(4):
            @pl.when(flags(j, part[0])[d])
            def _(d=d):
                act(e_copy(j, h, part, nbrs[d][1], d))

    def pair(bufs, sems, src, dst, i, j, dev):
        return [pltpu.make_async_remote_copy(
            src_ref=bufs[q].at[src], dst_ref=bufs[q + 2].at[dst], send_sem=sems[q].at[i], recv_sem=sems[q + 2].at[j],
            device_id={"col": dev}, device_id_type=MESH) for q in range(2)]

    def far_slot(j):
        return (j - (m + 1) * 2 * J + 2 * NR) % NR

    def half_copies(slot):
        return pair(half_bufs, half_sems, slot, slot, slot, slot, sibling)

    def mate_copies(jj):
        return pair(mate_bufs, mate_sems, jj, jj, jj, jj, sibling)

    def far_copies(j):
        slot, md = far_slot(j), j // (2 * J)
        at = ((m - md - 1 + NCH) % NCH, j % J, k)
        return pair(far_bufs, far_sems, slot, at, slot, at, j // J)

    def encode(value, dst, scales, slot, row0, i):
        top = jnp.maximum(jnp.max(jnp.abs(value), axis=0, keepdims=True), 1e-30)
        scales[slot, pl.ds(i, 1), :] = top * (1.0 / 32767.0)
        dst[slot, pl.ds(pl.multiple_of(row0, MB), MB), :] = jnp.round(value * (32767.0 / top)).astype(jnp.int16)

    def compute(j):
        jj, d = j % J, j // J
        far = d // 2 != m
        slot = far_slot(j)

        def rows_of(half, keep):
            def chunk(i, carry):
                row0 = half * HM + i * MM
                prod = jnp.dot(AC[pl.ds(pl.multiple_of(row0, MM), MM), :], E[j], preferred_element_type=jnp.float32)
                for o in range(J):
                    @pl.when(j == c * J + o)
                    def _(o=o):
                        out_ref[pl.ds(pl.multiple_of(row0, MM), MM), o * w:(o + 1) * w] = prod

                @pl.when(d == sibling)
                def _():
                    for u in range(MM // MB):
                        encode(prod[u * MB:(u + 1) * MB], mate_bufs[0], mate_bufs[1], jj, row0 + u * MB, row0 // MB + u)

                @pl.when(far)
                def _():
                    if keep:
                        Y[pl.ds(pl.multiple_of(i * MM, MM), MM), :] = prod
                    else:
                        for u in range(MM // MB):
                            encode(prod[u * MB:(u + 1) * MB], half_bufs[0], half_bufs[1], slot,
                                   i * MM + u * MB, i * (MM // MB) + u)
                return carry

            lax.fori_loop(0, HM // MM, chunk, 0)

        rows_of(1 - k, False)

        @pl.when(far)
        def _():
            for cp in half_copies(slot):
                cp.start()

        rows_of(k, True)

        @pl.when(d == sibling)
        def _():
            for cp in mate_copies(jj):
                cp.start()

        @pl.when(far)
        def _():
            for cp in half_copies(slot):
                cp.wait_recv()

            def chunk(i, carry):
                rows = pl.ds(pl.multiple_of(i * MB, MB), MB)
                value = Y[rows, :] + half_bufs[2][slot, rows, :].astype(jnp.float32) * half_bufs[3][slot, pl.ds(i, 1), :]
                encode(value, far_bufs[0], far_bufs[1], slot, i * MB, i)
                return carry

            lax.fori_loop(0, HM // MB, chunk, 0)
            for cp in far_copies(j):
                cp.start()

    for h in range(H):
        for dm in range(1, NCH):
            src = (m + dm) % NCH * 2 + k
            g_copy(h, src, sibling, 0).wait_recv()
            g_copy(h, src, sibling, NCH - 1 + dm).start()
        for dm in range(NCH):
            g_copy(h, (m + dm) % NCH * 2 + 1 - k, sibling, 0).wait_recv()
        for q in range(CAP):
            E[r, q * BS:(q + 1) * BS, h * wh:(h + 1) * wh] = G[h][pos[q]]
        for part in PARTS:
            forward(r, h, part, lambda cp: cp.start())
    compute(r)

    def zorder(i):
        near = jnp.minimum(z, NZ - 1 - z)
        t = (i + 1) // 2
        two = jnp.where(i % 2 == 1, z - t, z + t)
        one = jnp.where(z < NZ - 1 - z, z + (i - near), z - (i - near))
        return jnp.where(i <= 2 * near, two, one)

    def xorder(i):
        near = jnp.minimum(x, NX - 1 - x)
        t = (i + 1) // 2
        two = jnp.where(i % 2 == 1, x - t, x + t)
        one = jnp.where(x < NX - 1 - x, x + (i - near), x - (i - near))
        return jnp.where(i <= 2 * near, two, one)

    def step(s, carry):
        if NX == 2:
            last = s == 2 * NZ - 1
            d = jnp.where(last, 1, (s + 1) % 2)
            zi = jnp.where(last, NZ - 1, jnp.where(s % 2 == 1, (s + 1) // 2, s // 2 - 1))
            j = zorder(zi) * NX + jnp.where(d == 1, 1 - x, x)
        else:
            j = zorder(s // NX) * NX + xorder(s % NX)
        for h in range(H):
            for part in PARTS:
                e_copy(j, h, part, nbrs[0][1], 0).wait_recv()
                forward(j, h, part, lambda cp: cp.start())
        compute(j)
        return carry

    lax.fori_loop(1, NR, step, 0)

    for jj in range(J):
        for cp in mate_copies(jj):
            cp.wait_recv()
        for rel in range(NCH - 1):
            for half in range(2):
                for cp in pair(far_bufs, far_sems, 0, (rel, jj, half), 0, (rel, jj, half), sibling):
                    cp.wait_recv()

        def add(i, carry, jj=jj):
            rows = pl.ds(pl.multiple_of(i * MB, MB), MB)
            half, ih = i // (HM // MB), i % (HM // MB)
            inner = pl.ds(pl.multiple_of(ih * MB, MB), MB)
            total = out_ref[rows, jj * w:(jj + 1) * w]
            total += mate_bufs[2][jj, rows, :].astype(jnp.float32) * mate_bufs[3][jj, pl.ds(i, 1), :]
            for rel in range(NCH - 1):
                total += (far_bufs[2][rel, jj, half, inner, :].astype(jnp.float32)
                          * far_bufs[3][rel, jj, half, pl.ds(ih, 1), :])
            out_ref[rows, jj * w:(jj + 1) * w] = total
            return carry
        lax.fori_loop(0, M // MB, add, 0)

    for h in range(H):
        for idx in range(NC - 1):
            g_copy(h, c, sibling, idx).wait_send()

    def drain(j, carry):
        for h in range(H):
            for part in PARTS:
                forward(j, h, part, lambda cp: cp.wait_send())

        @pl.when(j // (2 * J) != m)
        def _():
            for cp in half_copies(far_slot(j)) + far_copies(j):
                cp.wait_send()
        return carry

    for jj in range(J):
        for cp in mate_copies(jj):
            cp.wait_send()
    lax.fori_loop(0, NR, drain, 0)


def body(NR, NC, anc_inv, panel, structure):
    c = lax.axis_index("col")
    r = lax.axis_index("row")
    M, cols = anc_inv.shape
    GB = cols // BS
    CAP = GB * 3 // 4 + 1
    PB, w = panel.shape[1] // BS, panel.shape[2]
    NX = 2
    while NX * NX * 2 < NR:
        NX *= 2
    NZ = NR // NX
    H = max(1, w // 128)
    wh = w // H
    J = NR // NC
    HM = M // 2
    MB = 256
    MM = min(512, HM)
    RB = 256
    K = CAP * BS
    KA = (CAP - (CAP + 7) // 10) * BS
    s = structure[0]
    n = s.shape[0]
    at = jnp.arange(n, dtype=jnp.int32)
    mine = s // GB == c
    rank = jnp.sum((at[None, :] < at[:, None]) & mine[None, :], axis=1)
    hot = mine[None, :] & (rank[None, :] == jnp.arange(CAP)[:, None])
    pos = n + jnp.sum(jnp.where(hot, at[None, :] - n, 0), axis=1).astype(jnp.int32)
    ids = jnp.sum(jnp.where(hot, (s - c * GB)[None, :], 0), axis=1).astype(jnp.int32)
    D = pltpu.SemaphoreType.DMA
    far = NR - 2 * J
    lead = (NC // 2 - 1, J, 2)

    def bufs(send, recv, rows):
        chunks = max(8, rows // MB)
        return [pltpu.VMEM((*send, rows, w), jnp.int16), pltpu.VMEM((*send, chunks, w), jnp.float32),
                pltpu.VMEM((*recv, rows, w), jnp.int16), pltpu.VMEM((*recv, chunks, w), jnp.float32)]

    def sems(send, recv):
        return [D(send), D(send), D(recv), D(recv)]

    smem = pl.BlockSpec(memory_space=pltpu.SMEM)
    hbm = pl.BlockSpec(memory_space=pl.ANY)
    total = pl.pallas_call(
        functools.partial(kernel, (NZ, NX, NC, CAP, H, MB, MM, KA)),
        out_shape=jax.ShapeDtypeStruct((M, J * w), jnp.float32),
        in_specs=[smem, smem, hbm, hbm],
        out_specs=pl.BlockSpec(memory_space=pltpu.VMEM),
        scratch_shapes=[
            [pltpu.VMEM((NC * PB + 1, BS, wh), jnp.bfloat16)] * H,
            pltpu.VMEM((NR, K, w), jnp.bfloat16),
            pltpu.VMEM((M, K), jnp.bfloat16),
            [pltpu.VMEM((GB, RB, BS), jnp.bfloat16)] * 2,
            pltpu.VMEM((HM, w), jnp.float32),
            bufs((far,), lead, HM), bufs((J,), (J,), M), bufs((far,), (far,), HM),
            D((H,)), D((2, GB)), D((H, NC - 1)), D((H, NC)), D((NR, H, 2, 4)), D((NR, H, 2)),
            sems((far,), lead), sems((J,), (J,)), sems((far,), (far,)),
        ],
        compiler_params=pltpu.CompilerParams(
            collective_id=0, has_side_effects=True, vmem_limit_bytes=63 * 2**20),
    )(ids, pos, anc_inv, panel.reshape(1, PB, BS, w))
    own_blocks = r * (M // BS) + jnp.arange(M // BS, dtype=jnp.int32)
    member = jnp.any(s[None, :] == own_blocks[:, None], axis=1)
    mask = jnp.repeat(member, BS)
    return jnp.where(mask[:, None], -total, 0.0)[None]


def solution(mesh):
    in_specs = (P("row", "col"), P(None, "col", "row"), P())
    out_specs = P(None, "row", "col")
    fn = functools.partial(body, mesh.shape["row"], mesh.shape["col"])
    return jax.shard_map(fn, mesh=mesh, in_specs=in_specs, out_specs=out_specs, check_vma=False)
```
